256 devices in a mesh: seq: 64 (over x, z, core), chan: 4 (over y).
Axes of the slice: x: 4, y: 4, z: 8, core: 2. Of those that a mesh axis runs over, the one named last changes fastest.
Arguments:
- q_gate: bfloat16 [32768, 1024], P('seq', 'chan'), may hold values from -6 to 6
- k_gate: bfloat16 [32768, 1024], P('seq', 'chan'), may hold values from -6 to 6
- value: bfloat16 [32768, 1024], P('seq', 'chan'), may hold values from -6 to 6
- decay: float32 [16, 1024], P(None, 'chan'), may hold values from 7.6293945e-06 to 0.0333333333
- residue: float32 [16, 1024], P(None, 'chan'), may hold values from -1 to 1
- skip: float32 [1024], P('chan'), may hold values from -1 to 1
- out_weight: bfloat16 [1024, 1024], P(None, 'chan'), may hold values from -0.1875 to 0.1875
- out_bias: float32 [1024], P('chan'), may hold values from -3 to 3
Outputs:
- layer_out: bfloat16 [32768, 1024], P('seq', 'chan')
The draws below stay inside these ranges and needn't reach their ends.
All inputs are finite; a program needn't handle non-finite values.
Results may differ from the reference program's by a relative error of at most 0.015.
Values may be sent and summed in bfloat16 or wider, within the bound.
A program may use at most 64 MiB of HBM per device.

```python
import jax
import jax.numpy as jnp
from jax import lax

CH = 1024
MODES = 16
SEQ_LEN = 32768


def mode_lengths(key, shortest, longest):
    spread = jax.random.uniform(key, (MODES, CH), jnp.float32)
    return jnp.exp(jnp.log(shortest) + spread * (jnp.log(longest) - jnp.log(shortest)))


def draw_decay(key, part):
    lengths = mode_lengths(key, 30.0, 4.0 * SEQ_LEN)
    return 1.0 / lengths


def draw_residue(key, part):
    lengths = mode_lengths(key, 30.0, 4.0 * SEQ_LEN)
    key = jax.random.fold_in(key, 7)
    scales = jnp.clip(jax.random.normal(key, (MODES, CH), jnp.float32), -4.0, 4.0)
    return scales * jnp.sqrt(2.0 / (MODES * jnp.minimum(lengths, 1.0 * SEQ_LEN)))


def level_of(rng, dims, cuts, least, largest):
    def one(axis_at, shards_of):
        steps = jax.random.uniform(jax.random.fold_in(jax.random.fold_in(rng, 6), axis_at), (shards_of,), jnp.float32, least / len(cuts), largest / len(cuts))
        return jnp.repeat(jnp.exp(steps), dims[axis_at] // shards_of).reshape((-1,) + (1,) * (len(dims) - axis_at - 1))

    gain = one(*cuts[0])
    for cut in cuts[1:]:
        gain = gain * one(*cut)
    return gain


def scatter_about(rng, extent, width, bound, split=(), kind=jnp.bfloat16):
    gain = level_of(rng, extent, split, -0.22, 0.18) if split else 1.0
    drawn = jax.random.normal(rng, extent, jnp.float32) * width * gain
    return jnp.minimum(jnp.maximum(drawn, -bound), bound).astype(kind)


def setup_inputs(seed: int = 0) -> dict:
    keys = jax.random.split(jax.random.key(seed), 9)
    return {
        "q_gate": scatter_about(keys[0], (SEQ_LEN, CH), 1.0, 6.0, ((0, 64), (1, 4))),
        "k_gate": scatter_about(keys[1], (SEQ_LEN, CH), 1.0, 6.0, ((0, 64), (1, 4))),
        "value": scatter_about(keys[2], (SEQ_LEN, CH), 1.0, 6.0, ((0, 64), (1, 4))),
        "decay": draw_decay(jax.random.fold_in(keys[8], 71), 0),
        "residue": draw_residue(jax.random.fold_in(keys[8], 71), 0),
        "skip": jnp.clip(jax.random.uniform(keys[5], (CH,), jnp.float32, -1.0, 1.0) * level_of(keys[5], (CH,), ((0, 4),), -0.4, 0.0), -1.0, 1.0),
        "out_weight": scatter_about(keys[6], (CH, CH), CH ** -0.5, 0.1875, ((1, 4),)),
        "out_bias": scatter_about(keys[7], (CH,), 0.5, 3.0, ((0, 4),), jnp.float32),
    }


def reference(q_gate, k_gate, value, decay, residue, skip, out_weight, out_bias):
    gated = (k_gate.astype(jnp.float32) * value.astype(jnp.float32)).astype(jnp.bfloat16)
    block_width = min(CH, 128)
    group_count = CH // block_width
    padded_len = 2 * SEQ_LEN
    positions = jnp.arange(SEQ_LEN).astype(jnp.float32)

    def one_group(group_index):
        offset = (group_index * block_width).astype(jnp.int32)
        signal = lax.dynamic_slice_in_dim(gated, offset, block_width, 1).astype(jnp.float32)
        rate_block = lax.dynamic_slice_in_dim(decay, offset, block_width, 1)
        weight_block = lax.dynamic_slice_in_dim(residue, offset, block_width, 1)
        kernel = jnp.zeros((SEQ_LEN, block_width), jnp.float32)
        for order_index in range(MODES):
            kernel = kernel + weight_block[order_index] * jnp.exp(-rate_block[order_index] * positions[:, None])
        spectrum = jnp.fft.rfft(signal, n=padded_len, axis=0) * jnp.fft.rfft(kernel, n=padded_len, axis=0)
        return jnp.fft.irfft(spectrum, n=padded_len, axis=0)[:SEQ_LEN].astype(jnp.float32)

    blocks = lax.map(one_group, jnp.arange(group_count, dtype=jnp.int32))
    convolved = jnp.transpose(blocks, (1, 0, 2)).reshape(SEQ_LEN, CH)
    modulated = (q_gate.astype(jnp.float32) * (convolved + skip * gated.astype(jnp.float32))).astype(jnp.bfloat16)
    projected = jnp.dot(modulated, out_weight, preferred_element_type=jnp.float32) + out_bias
    return projected.astype(jnp.bfloat16)
```

```python
import functools

import jax
import jax.numpy as jnp
from jax import lax
from jax.experimental import pallas as pl
from jax.experimental.pallas import tpu as pltpu
from jax.sharding import PartitionSpec as P

MESH = pl.DeviceIdType.MESH
F32 = jnp.float32
BF16 = jnp.bfloat16
NX, NZ, NC, NY = 4, 8, 2, 4
SUB = 8
LANES = 128
CHUNKS = 4


def rows_of(array, n, lane):
    return jnp.broadcast_to(array[n : n + 1, lane : lane + LANES], (SUB, LANES))


def kernel(
    q_hbm, k_hbm, v_hbm, decay_ref, residue_ref, skip_ref, w_hbm, bias_ref, out_ref,
    k_buf, v_buf, q_buf, w_buf, u_buf, qf_buf, y_buf, h_buf, lam_buf, sub_buf, g_buf,
    z_buf, x_buf, mate_s, mate_pre, t_buf, p_buf, gathered, o_buf,
    load_sem, z_send, z_recv, x_send, x_recv, mate_send, mate_recv, y_send, y_recv,
):
    modes, channels = decay_ref.shape
    tokens = u_buf.shape[1]
    steps = tokens // SUB
    part = steps // CHUNKS
    lane_starts = range(0, channels, LANES)
    seq = lax.axis_index("seq")
    y = lax.axis_index("chan")
    x, z, core = seq // (NZ * NC), (seq // NC) % NZ, seq % NC

    def device(xx, zz, cc, yy):
        return ((xx * NZ + zz) * NC + cc, yy)

    loads = [
        pltpu.make_async_copy(src, dst, load_sem.at[i])
        for i, (src, dst) in enumerate(
            [(k_hbm, k_buf), (v_hbm, v_buf), (q_hbm, q_buf), (w_hbm, w_buf)]
        )
    ]
    for load in loads:
        load.start()

    x_buf[...] = jnp.zeros_like(x_buf)
    barrier = pltpu.get_barrier_semaphore()
    partners = [device(x, z, 1 - core, y)]
    z_order = (4, 3, 5, 2, 6, 1, 7)
    partners += [device(x, (z + k) % NZ, core, y) for k in z_order]
    partners += [device((x + k) % NX, z, cc, y) for k in range(1, NX) for cc in range(NC)]
    partners += [device(x, z, core, (y + k) % NY) for k in range(1, NY)]
    for partner in partners:
        pl.semaphore_signal(barrier, inc=1, device_id=partner, device_id_type=MESH)

    decay = decay_ref[...]
    lam_buf[...] = jnp.exp(-decay)

    loads[0].wait()
    loads[1].wait()
    for lane in lane_starts:
        k_part, v_part = (buf[:, pl.ds(lane, LANES)].astype(F32) for buf in (k_buf, v_buf))
        u_buf[lane // LANES] = (k_part * v_part).astype(BF16).astype(F32)

    sublane = lax.broadcasted_iota(jnp.int32, (SUB, LANES), 0)
    for lane in lane_starts:
        lam = [rows_of(lam_buf[...], n, lane) for n in range(modes)]

        def advance(b, state, lam=lam, lane=lane):
            u = u_buf[lane // LANES, pl.ds(b, SUB, stride=steps), :]
            return tuple(l * h + u for l, h in zip(lam, state))

        zero = jnp.zeros((SUB, LANES), F32)
        state = lax.fori_loop(0, steps, advance, (zero,) * modes, unroll=8)
        for n in range(modes):
            run = state[n]
            for shift in (1, 2, 4):
                factor = jnp.exp(-rows_of(decay, n, lane) * float(steps * shift))
                moved = jnp.where(sublane >= shift, pltpu.roll(run, shift, 0), 0.0)
                run = run + factor * moved
            z_buf[pl.ds(z, 1), pl.ds(n, 1), pl.ds(lane, LANES)] = run[SUB - 1 : SUB].reshape(1, 1, LANES)
            h_buf[n, :, pl.ds(lane, LANES)] = jnp.where(sublane >= 1, pltpu.roll(run, 1, 0), 0.0)

    pl.semaphore_wait(barrier, len(partners))

    z_copies = [
        pltpu.make_async_remote_copy(
            src_ref=z_buf.at[z], dst_ref=z_buf.at[z],
            send_sem=z_send.at[i], recv_sem=z_recv.at[z],
            device_id=device(x, (z + k) % NZ, core, y), device_id_type=MESH,
        )
        for i, k in enumerate(z_order)
    ]
    for copy in z_copies:
        copy.start()
    mate = device(x, z, 1 - core, y)
    s_copy = pltpu.make_async_remote_copy(
        src_ref=z_buf.at[z], dst_ref=mate_s, send_sem=mate_send.at[0], recv_sem=mate_recv.at[0],
        device_id=mate, device_id_type=MESH,
    )
    s_copy.start()

    for lane in lane_starts:
        lam = [rows_of(lam_buf[...], n, lane) for n in range(modes)]
        weight = [rows_of(residue_ref[...], n, lane) for n in range(modes)]
        skip_row = jnp.broadcast_to(skip_ref[:, lane : lane + LANES], (SUB, LANES))

        def local(b, state, lam=lam, weight=weight, skip_row=skip_row, lane=lane):
            u = u_buf[lane // LANES, pl.ds(b, SUB, stride=steps), :]
            state = tuple(l * h + u for l, h in zip(lam, state))
            total = [w * h for w, h in zip(weight, state)] + [skip_row * u]
            while len(total) > 1:
                total = [a + c for a, c in zip(total[::2], total[1::2])] + total[len(total) // 2 * 2 :]
            y_buf[b, :, pl.ds(lane, LANES)] = total[0]
            return state

        first = tuple(h_buf[n, :, pl.ds(lane, LANES)] for n in range(modes))
        lax.fori_loop(0, steps, local, first, unroll=2)
        for n in range(modes):
            place = (sublane * steps + 1).astype(F32)
            sub_buf[n, :, pl.ds(lane, LANES)] = weight[n] * jnp.exp(-rows_of(decay, n, lane) * place)
    loads[2].wait()
    for lane in lane_starts:
        qf_buf[lane // LANES] = q_buf[:, pl.ds(lane, LANES)].astype(F32)

    chip_power = jnp.exp(-decay * float(NC * tokens))
    row_power = jnp.exp(-decay * float(NZ * NC * tokens))
    half_power = jnp.exp(-decay * float(tokens))
    place_power = jnp.exp(-decay * (z * (NC * tokens)).astype(F32))

    for copy in z_copies:
        copy.wait_send()
    for k in range(1, NZ):
        src = (z + k) % NZ
        pltpu.make_async_remote_copy(
            src_ref=z_buf.at[src], dst_ref=z_buf.at[src], send_sem=z_send.at[0],
            recv_sem=z_recv.at[src], device_id=mate, device_id_type=MESH,
        ).wait_recv()
    total = jnp.zeros_like(decay)
    prefix = jnp.zeros_like(decay)
    for zz in range(NZ):
        prefix = jnp.where(z == zz, total, prefix)
        total = chip_power * total + z_buf[zz]
    t_buf[...] = total
    p_buf[...] = prefix

    for k in range(1, NX):
        @pl.when(x + k < NX)
        def _(k=k):
            for cc in range(NC):
                pltpu.make_async_remote_copy(
                    src_ref=t_buf, dst_ref=x_buf.at[core, x],
                    send_sem=x_send.at[k - 1, cc], recv_sem=x_recv.at[core, x],
                    device_id=device(x + k, z, cc, y), device_id_type=MESH,
                ).start()
    p_copy = pltpu.make_async_remote_copy(
        src_ref=p_buf, dst_ref=mate_pre, send_sem=mate_send.at[1], recv_sem=mate_recv.at[1],
        device_id=mate, device_id_type=MESH,
    )
    p_copy.start()
    s_copy.wait()
    p_copy.wait()
    for k in range(1, NX):
        @pl.when(x >= k)
        def _(k=k):
            for cc in range(NC):
                pltpu.make_async_remote_copy(
                    src_ref=t_buf, dst_ref=x_buf.at[cc, x - k],
                    send_sem=x_send.at[0, 0], recv_sem=x_recv.at[cc, x - k],
                    device_id=mate, device_id_type=MESH,
                ).wait_recv()

    before = jnp.zeros_like(decay)
    for xx in range(NX - 1):
        step = half_power * x_buf[0, xx] + x_buf[1, xx]
        before = jnp.where(xx < x, row_power * before + step, before)
    other = mate_pre[...]
    early = jnp.where(core == 0, prefix, other)
    late = jnp.where(core == 0, other, prefix)
    carry = place_power * before + half_power * early + late
    carry = jnp.where(core == 0, carry, half_power * carry + mate_s[...])
    g_buf[...] = carry

    y_copies = []
    for lane in lane_starts:
        for n in range(modes):
            h_buf[n, :, pl.ds(lane, LANES)] = sub_buf[n, :, pl.ds(lane, LANES)] * rows_of(g_buf[...], n, lane)
    for j in range(CHUNKS):
        for lane in lane_starts:
            lam = [rows_of(lam_buf[...], n, lane) for n in range(modes)]

            def finish(i, state, lam=lam, lane=lane, j=j):
                pair = []
                for o in range(2):
                    b = j * part + 2 * i + o
                    total = list(state) + [y_buf[b, :, pl.ds(lane, LANES)]]
                    while len(total) > 1:
                        total = [a + c for a, c in zip(total[::2], total[1::2])] + total[len(total) // 2 * 2 :]
                    gate = qf_buf[lane // LANES, pl.ds(b, SUB, stride=steps), :]
                    pair.append(gate * total[0])
                    state = tuple(l * h for l, h in zip(lam, state))
                rows = jnp.concatenate(pair, axis=0).astype(BF16)
                start = pl.multiple_of(i * 2 * SUB, 2 * SUB)
                gathered[y, j, pl.ds(start, 2 * SUB), pl.ds(lane, LANES)] = rows
                return state

            first = tuple(h_buf[n, :, pl.ds(lane, LANES)] for n in range(modes))
            last = lax.fori_loop(0, part // 2, finish, first)
            for n in range(modes):
                h_buf[n, :, pl.ds(lane, LANES)] = last[n]
        for i, k in enumerate((2, 1, 3)):
            copy = pltpu.make_async_remote_copy(
                src_ref=gathered.at[y, j], dst_ref=gathered.at[y, j],
                send_sem=y_send.at[i, j], recv_sem=y_recv.at[y, j],
                device_id=device(x, z, core, (y + k) % NY), device_id_type=MESH,
            )
            copy.start()
            y_copies.append(copy)

    loads[3].wait()
    bias = jnp.broadcast_to(bias_ref[...], (part * SUB, channels))
    for j in range(CHUNKS):
        for k in range(1, NY):
            src = (y + k) % NY
            pltpu.make_async_remote_copy(
                src_ref=gathered.at[src, j], dst_ref=gathered.at[src, j],
                send_sem=y_send.at[0, 0], recv_sem=y_recv.at[src, j],
                device_id=mate, device_id_type=MESH,
            ).wait_recv()
        projected = bias
        for yy in range(NY):
            projected = projected + jnp.dot(
                gathered[yy, j], w_buf[pl.ds(yy * channels, channels), :], preferred_element_type=F32
            )
        for i in range(part):
            for lane in lane_starts:
                o_buf[lane // LANES, pl.ds(j * part + i, SUB, stride=steps), :] = projected[
                    i * SUB : (i + 1) * SUB, lane : lane + LANES
                ]
    for lane in lane_starts:
        out_ref[:, pl.ds(lane, LANES)] = o_buf[lane // LANES].astype(BF16)

    for copy in y_copies:
        copy.wait_send()
    for k in range(1, NX):
        @pl.when(x + k < NX)
        def _(k=k):
            for cc in range(NC):
                pltpu.make_async_remote_copy(
                    src_ref=t_buf, dst_ref=x_buf.at[core, x],
                    send_sem=x_send.at[k - 1, cc], recv_sem=x_recv.at[core, x],
                    device_id=device(x + k, z, cc, y), device_id_type=MESH,
                ).wait_send()


def layer(q_gate, k_gate, value, decay, residue, skip, out_weight, out_bias):
    tokens, channels = q_gate.shape
    modes = decay.shape[0]
    part_rows = tokens // CHUNKS
    dma = pltpu.SemaphoreType.DMA
    state = (modes, channels)
    any_spec = pl.BlockSpec(memory_space=pl.ANY)
    vmem = pl.BlockSpec(memory_space=pltpu.VMEM)
    return pl.pallas_call(
        kernel,
        out_shape=jax.ShapeDtypeStruct((tokens, channels), BF16),
        in_specs=[any_spec, any_spec, any_spec, vmem, vmem, vmem, any_spec, vmem],
        out_specs=vmem,
        scratch_shapes=[
            pltpu.VMEM((tokens, channels), BF16),
            pltpu.VMEM((tokens, channels), BF16),
            pltpu.VMEM((tokens, channels), BF16),
            pltpu.VMEM(out_weight.shape, BF16),
            pltpu.VMEM((channels // LANES, tokens, LANES), F32),
            pltpu.VMEM((channels // LANES, tokens, LANES), F32),
            pltpu.VMEM((tokens // SUB, SUB, channels), F32),
            pltpu.VMEM((modes, SUB, channels), F32),
            pltpu.VMEM(state, F32),
            pltpu.VMEM((modes, SUB, channels), F32),
            pltpu.VMEM(state, F32),
            pltpu.VMEM((NZ,) + state, F32),
            pltpu.VMEM((NC, NX) + state, F32),
            pltpu.VMEM(state, F32),
            pltpu.VMEM(state, F32),
            pltpu.VMEM(state, F32),
            pltpu.VMEM(state, F32),
            pltpu.VMEM((NY, CHUNKS, part_rows, channels), BF16),
            pltpu.VMEM((channels // LANES, tokens, LANES), F32),
            dma((4,)), dma((NZ - 1,)), dma((NZ,)), dma((NX - 1, NC)), dma((NC, NX)),
            dma((2,)), dma((2,)), dma((NY - 1, CHUNKS)), dma((NY, CHUNKS)),
        ],
        compiler_params=pltpu.CompilerParams(
            collective_id=0, has_side_effects=True, vmem_limit_bytes=32 * 2**20
        ),
        name="layer",
    )(q_gate, k_gate, value, decay, residue, skip.reshape(1, -1), out_weight, out_bias.reshape(1, -1))


def solution(mesh):
    return jax.shard_map(
        layer,
        mesh=mesh,
        in_specs=(
            P("seq", "chan"),
            P("seq", "chan"),
            P("seq", "chan"),
            P(None, "chan"),
            P(None, "chan"),
            P("chan"),
            P(None, "chan"),
            P("chan"),
        ),
        out_specs=P("seq", "chan"),
        check_vma=False,
    )
```

```python
import functools

import jax
import jax.numpy as jnp
from jax import lax
from jax.experimental import pallas as pl
from jax.experimental.pallas import tpu as pltpu
from jax.sharding import PartitionSpec as P

MESH = pl.DeviceIdType.MESH
F32 = jnp.float32
BF16 = jnp.bfloat16
NX, NZ, NC, NY = 4, 8, 2, 4
SUB = 8
LANES = 128
CHUNKS = 8
EARLY = 4


def tree(terms):
    while len(terms) > 1:
        terms = [a + b for a, b in zip(terms[::2], terms[1::2])] + terms[len(terms) // 2 * 2 :]
    return terms[0]


def rows_of(array, n, lane):
    return jnp.broadcast_to(array[n : n + 1, lane : lane + LANES], (SUB, LANES))


def kernel(
    q_hbm, k_hbm, v_hbm, decay_hbm, residue_hbm, skip_hbm, w_hbm, bias_hbm, out_ref,
    decay_ref, residue_ref, skip_ref, bias_ref, k_buf, v_buf, q_buf, w_buf, u_buf, qf_buf, y_buf, h_buf, lam_buf, sub_buf,
    q_peer, y_peer, d_peer, c_peer, g_peer,
    z_buf, x_buf, mate_s, mate_pre, t_buf, p_buf, gathered, o_buf,
    load_sem, z_ready, x_ready, z_send, z_recv, x_send, x_recv, mate_send, mate_recv, y_send, y_recv,
    d_send, d_recv, q_send, q_recv, l_send, l_recv, c_send, c_recv,
):
    modes, channels = decay_ref.shape
    tokens = u_buf.shape[1]
    steps = tokens // SUB
    part = steps // CHUNKS
    early = EARLY * part
    lane_starts = range(0, channels, LANES)
    seq = lax.axis_index("seq")
    y = lax.axis_index("chan")
    x, z, core = seq // (NZ * NC), (seq // NC) % NZ, seq % NC

    def device(xx, zz, cc, yy):
        return ((xx * NZ + zz) * NC + cc, yy)

    loads = [
        pltpu.make_async_copy(src, dst, load_sem.at[i])
        for i, (src, dst) in enumerate(
            [
                (k_hbm, k_buf), (v_hbm, v_buf), (decay_hbm, decay_ref), (residue_hbm, residue_ref),
                (skip_hbm, skip_ref), (q_hbm, q_buf), (w_hbm, w_buf), (bias_hbm, bias_ref),
            ]
        )
    ]
    for load in loads:
        load.start()

    x_buf[...] = jnp.zeros_like(x_buf)
    z_buf[...] = jnp.zeros_like(z_buf)
    mate = device(x, z, 1 - core, y)
    y_peers = [device(x, z, core, (y + k) % NY) for k in (2, 1, 3)]
    barrier = pltpu.get_barrier_semaphore()

    def tell(semaphore, where):
        pl.semaphore_signal(semaphore, inc=1, device_id=where, device_id_type=MESH)

    for where in y_peers + [mate]:
        tell(barrier, where)
    for k in range(1, NZ):
        @pl.when(z + k < NZ)
        def _(k=k):
            tell(barrier, device(x, z + k, core, y))
    for k in range(1, NX):
        @pl.when(x + k < NX)
        def _(k=k):
            for cc in range(NC):
                tell(barrier, device(x + k, z, cc, y))
    pl.semaphore_wait(barrier, NY + z + NC * x)
    for k in range(1, NZ):
        @pl.when(z >= k)
        def _(k=k):
            tell(z_ready.at[z], device(x, z - k, core, y))
    for k in range(1, NX):
        @pl.when(x >= k)
        def _(k=k):
            for cc in range(NC):
                tell(x_ready.at[x, core], device(x - k, z, cc, y))

    def along_y(src, dst, send, recv):
        copies = [
            pltpu.make_async_remote_copy(
                src_ref=src, dst_ref=dst, send_sem=send.at[i], recv_sem=recv.at[y],
                device_id=where, device_id_type=MESH,
            )
            for i, where in enumerate(y_peers)
        ]
        for copy in copies:
            copy.start()
        y_copies.extend(copies)

    def from_y(src, dst, recv):
        pltpu.make_async_remote_copy(
            src_ref=dst, dst_ref=dst, send_sem=q_send.at[0], recv_sem=recv.at[src],
            device_id=mate, device_id_type=MESH,
        ).wait_recv()

    y_copies = []
    others = [(y + k) % NY for k in (1, 3, 2)]
    along_y(q_hbm.at[:, pl.ds(0, early)], q_peer.at[y], q_send, q_recv)

    loads[2].wait()
    decay = decay_ref[...]
    d_peer[y] = decay
    along_y(d_peer.at[y], d_peer.at[y], d_send, d_recv)
    lam_buf[y] = jnp.exp(-decay)

    loads[0].wait()
    loads[1].wait()
    for lane in lane_starts:
        k_part, v_part = (buf[:, pl.ds(lane, LANES)].astype(F32) for buf in (k_buf, v_buf))
        u_buf[lane // LANES] = (k_part * v_part).astype(BF16).astype(F32)

    sublane = lax.broadcasted_iota(jnp.int32, (SUB, LANES), 0)
    for lane in lane_starts:
        lam = [rows_of(lam_buf[y], n, lane) for n in range(modes)]

        def advance(b, state, lam=lam, lane=lane):
            u = u_buf[lane // LANES, pl.ds(b, SUB, stride=steps), :]
            return tuple(l * h + u for l, h in zip(lam, state))

        zero = jnp.zeros((SUB, LANES), F32)
        state = lax.fori_loop(0, steps, advance, (zero,) * modes, unroll=8)
        for n in range(modes):
            run = state[n]
            for shift in (1, 2, 4):
                factor = jnp.exp(-rows_of(decay, n, lane) * float(steps * shift))
                moved = jnp.where(sublane >= shift, pltpu.roll(run, shift, 0), 0.0)
                run = run + factor * moved
            z_buf[pl.ds(z, 1), pl.ds(n, 1), pl.ds(lane, LANES)] = run[SUB - 1 : SUB].reshape(1, 1, LANES)
            h_buf[n, :, pl.ds(lane, LANES)] = jnp.where(sublane >= 1, pltpu.roll(run, 1, 0), 0.0)

    def state_copy(slot, target):
        return pltpu.make_async_remote_copy(
            src_ref=z_buf.at[slot], dst_ref=z_buf.at[slot],
            send_sem=z_send.at[target], recv_sem=z_recv.at[slot],
            device_id=device(x, target, core, y), device_id_type=MESH,
        )

    def send_forward(k):
        pl.semaphore_wait(z_ready.at[z + k], 1)
        state_copy(z, z + k).start()

    needs_total = x < NX - 1
    half = NZ // 2
    s_copy = pltpu.make_async_remote_copy(
        src_ref=z_buf.at[z], dst_ref=mate_s, send_sem=mate_send.at[0], recv_sem=mate_recv.at[0],
        device_id=mate, device_id_type=MESH,
    )
    for k in (4, 3, 5, 2, 6, 1, 7):
        @pl.when((z >= k) & needs_total)
        def _(k=k):
            state_copy(z, z - k).start()
    for k in range(1, half):
        @pl.when((z + k < half) | ((z >= half) & (z + k < NZ)))
        def _(k=k):
            send_forward(k)
    s_copy.start()

    loads[3].wait()
    loads[4].wait()
    for lane in lane_starts:
        lam = [rows_of(lam_buf[y], n, lane) for n in range(modes)]
        weight = [rows_of(residue_ref[...], n, lane) for n in range(modes)]
        skip_row = jnp.broadcast_to(skip_ref[:, lane : lane + LANES], (SUB, LANES))

        def local(b, state, lam=lam, weight=weight, skip_row=skip_row, lane=lane):
            u = u_buf[lane // LANES, pl.ds(b, SUB, stride=steps), :]
            state = tuple(l * h + u for l, h in zip(lam, state))
            y_buf[b, :, pl.ds(lane, LANES)] = tree([w * h for w, h in zip(weight, state)] + [skip_row * u])
            return state

        first = tuple(h_buf[n, :, pl.ds(lane, LANES)] for n in range(modes))
        last = lax.fori_loop(0, early, local, first, unroll=4)
        y_peer[y, :, pl.ds(lane, LANES)] = (
            y_buf[pl.ds(0, early), :, pl.ds(lane, LANES)].reshape(early * SUB, LANES).astype(BF16)
        )
        for n in range(modes):
            h_buf[n, :, pl.ds(lane, LANES)] = last[n]
    along_y(y_peer.at[y], y_peer.at[y], l_send, l_recv)
    for lane in lane_starts:
        lam = [rows_of(lam_buf[y], n, lane) for n in range(modes)]
        weight = [rows_of(residue_ref[...], n, lane) for n in range(modes)]
        skip_row = jnp.broadcast_to(skip_ref[:, lane : lane + LANES], (SUB, LANES))

        def local(b, state, lam=lam, weight=weight, skip_row=skip_row, lane=lane):
            u = u_buf[lane // LANES, pl.ds(b, SUB, stride=steps), :]
            state = tuple(l * h + u for l, h in zip(lam, state))
            y_buf[b, :, pl.ds(lane, LANES)] = tree([w * h for w, h in zip(weight, state)] + [skip_row * u])
            return state

        first = tuple(h_buf[n, :, pl.ds(lane, LANES)] for n in range(modes))
        lax.fori_loop(early, steps, local, first, unroll=4)
        for n in range(modes):
            place = (sublane * steps + 1).astype(F32)
            sub_buf[y, n, :, pl.ds(lane, LANES)] = jnp.exp(-rows_of(decay, n, lane) * place)
    for k in range(1, NZ):
        @pl.when((z < half) & (z + k >= half) & (z + k < NZ))
        def _(k=k):
            send_forward(k)
    loads[5].wait()
    for lane in lane_starts:
        qf_buf[y, lane // LANES] = q_buf[:, :, pl.ds(lane, LANES)].astype(F32).reshape(tokens, LANES)

    chip_power = jnp.exp(-decay * float(NC * tokens))
    row_power = jnp.exp(-decay * float(NZ * NC * tokens))
    half_power = jnp.exp(-decay * float(tokens))
    place_power = jnp.exp(-decay * (z * (NC * tokens)).astype(F32))

    for k in range(1, NZ):
        @pl.when(z >= k)
        def _(k=k):
            state_copy(z - k, z).wait_recv()

        @pl.when((z + k < NZ) & needs_total)
        def _(k=k):
            state_copy(z + k, z).wait_recv()
    total = jnp.zeros_like(decay)
    prefix = jnp.zeros_like(decay)
    for zz in range(NZ):
        prefix = jnp.where(z == zz, total, prefix)
        total = chip_power * total + z_buf[zz]
    t_buf[...] = total
    p_buf[...] = prefix

    def total_copy(slot, target, cc):
        return pltpu.make_async_remote_copy(
            src_ref=t_buf, dst_ref=x_buf.at[core, slot],
            send_sem=x_send.at[target, cc], recv_sem=x_recv.at[core, slot],
            device_id=device(target, z, cc, y), device_id_type=MESH,
        )

    for k in range(1, NX):
        @pl.when(x + k < NX)
        def _(k=k):
            for cc in range(NC):
                pl.semaphore_wait(x_ready.at[x + k, cc], 1)
                total_copy(x, x + k, cc).start()
    p_copy = pltpu.make_async_remote_copy(
        src_ref=p_buf, dst_ref=mate_pre, send_sem=mate_send.at[1], recv_sem=mate_recv.at[1],
        device_id=mate, device_id_type=MESH,
    )
    p_copy.start()
    for src in others:
        from_y(src, q_peer.at[src], q_recv)
        from_y(src, d_peer.at[src], d_recv)
        lam_buf[src] = jnp.exp(-d_peer[src])
        for lane in lane_starts:
            for n in range(modes):
                place = (sublane * steps + 1).astype(F32)
                sub_buf[src, n, :, pl.ds(lane, LANES)] = jnp.exp(-rows_of(d_peer[src], n, lane) * place)
            for a in range(SUB):
                qf_buf[src, lane // LANES, pl.ds(a * steps, early), :] = q_peer[
                    src, a, :, pl.ds(lane, LANES)
                ].astype(F32)
    s_copy.wait()
    p_copy.wait()
    for k in range(1, NX):
        @pl.when(x >= k)
        def _(k=k):
            for cc in range(NC):
                pltpu.make_async_remote_copy(
                    src_ref=t_buf, dst_ref=x_buf.at[cc, x - k],
                    send_sem=x_send.at[0, 0], recv_sem=x_recv.at[cc, x - k],
                    device_id=mate, device_id_type=MESH,
                ).wait_recv()

    before = jnp.zeros_like(decay)
    for xx in range(NX - 1):
        step = half_power * x_buf[0, xx] + x_buf[1, xx]
        before = jnp.where(xx < x, row_power * before + step, before)
    other = mate_pre[...]
    first_core = jnp.where(core == 0, prefix, other)
    second_core = jnp.where(core == 0, other, prefix)
    carry = place_power * before + half_power * first_core + second_core
    carry = jnp.where(core == 0, carry, half_power * carry + mate_s[...])
    c_peer[y] = residue_ref[...] * carry
    along_y(c_peer.at[y], c_peer.at[y], c_send, c_recv)

    def start_carry(src):
        for lane in lane_starts:
            for n in range(modes):
                g_peer[n, :, pl.ds(lane, LANES)] = sub_buf[src, n, :, pl.ds(lane, LANES)] * rows_of(
                    c_peer[src], n, lane
                )

    def skip_early():
        for lane in lane_starts:
            for n in range(modes):
                ahead = jnp.exp(-rows_of(decay, n, lane) * float(early))
                g_peer[n, :, pl.ds(lane, LANES)] = g_peer[n, :, pl.ds(lane, LANES)] * ahead

    def finish(src, begin, end, local_at):
        for lane in lane_starts:
            lam = [rows_of(lam_buf[src], n, lane) for n in range(modes)]

            def step(i, state, lam=lam, lane=lane):
                b = begin + 2 * i
                local = local_at(b, lane)
                pair = []
                for o in range(2):
                    gate = qf_buf[src, lane // LANES, pl.ds(b + o, SUB, stride=steps), :]
                    pair.append(gate * tree(list(state) + [local[o]]))
                    state = tuple(l * h for l, h in zip(lam, state))
                rows = jnp.concatenate(pair, axis=0).astype(BF16)
                start = pl.multiple_of(b * SUB, 2 * SUB)
                gathered[src, pl.ds(start, 2 * SUB), pl.ds(lane, LANES)] = rows
                return state

            first = tuple(g_peer[n, :, pl.ds(lane, LANES)] for n in range(modes))
            last = lax.fori_loop(0, (end - begin) // 2, step, first, unroll=4)
            for n in range(modes):
                g_peer[n, :, pl.ds(lane, LANES)] = last[n]

    def own_local(b, lane):
        return [y_buf[b + o, :, pl.ds(lane, LANES)] for o in range(2)]

    def chunk_rows(j):
        return pl.ds(j * part * SUB, part * SUB)

    start_carry(y)
    skip_early()
    for j in range(EARLY, CHUNKS):
        finish(y, j * part, (j + 1) * part, own_local)
        for i, where in enumerate(y_peers):
            copy = pltpu.make_async_remote_copy(
                src_ref=gathered.at[y, chunk_rows(j)], dst_ref=gathered.at[y, chunk_rows(j)],
                send_sem=y_send.at[i, j], recv_sem=y_recv.at[y, j],
                device_id=where, device_id_type=MESH,
            )
            copy.start()
            y_copies.append(copy)
    start_carry(y)
    finish(y, 0, early, own_local)
    for src in others:
        from_y(src, y_peer.at[src], l_recv)
        from_y(src, c_peer.at[src], c_recv)
        start_carry(src)

        def sent_local(b, lane, src=src):
            start = pl.multiple_of(b * SUB, 2 * SUB)
            both = y_peer[src, pl.ds(start, 2 * SUB), pl.ds(lane, LANES)].astype(F32)
            return [both[:SUB], both[SUB:]]

        finish(src, 0, early, sent_local)

    loads[6].wait()
    loads[7].wait()
    bias = jnp.broadcast_to(bias_ref[...], (part * SUB, channels))
    for j in range(CHUNKS):
        if j >= EARLY:
            for src in others:
                pltpu.make_async_remote_copy(
                    src_ref=gathered.at[src, chunk_rows(j)], dst_ref=gathered.at[src, chunk_rows(j)],
                    send_sem=q_send.at[0], recv_sem=y_recv.at[src, j],
                    device_id=mate, device_id_type=MESH,
                ).wait_recv()
        projected = bias
        for yy in range(NY):
            projected = projected + jnp.dot(
                gathered[yy, chunk_rows(j), :], w_buf[pl.ds(yy * channels, channels), :], preferred_element_type=F32
            )
        for i in range(part):
            for lane in lane_starts:
                o_buf[lane // LANES, pl.ds(j * part + i, SUB, stride=steps), :] = projected[
                    i * SUB : (i + 1) * SUB, lane : lane + LANES
                ]
    for lane in lane_starts:
        out_ref[:, pl.ds(lane, LANES)] = o_buf[lane // LANES].astype(BF16)

    for copy in y_copies:
        copy.wait_send()
    for k in range(1, NZ):
        @pl.when(z + k < NZ)
        def _(k=k):
            state_copy(z, z + k).wait_send()

        @pl.when((z >= k) & needs_total)
        def _(k=k):
            state_copy(z, z - k).wait_send()
    for k in range(1, NX):
        @pl.when(x + k < NX)
        def _(k=k):
            for cc in range(NC):
                total_copy(x, x + k, cc).wait_send()


def layer(q_gate, k_gate, value, decay, residue, skip, out_weight, out_bias):
    tokens, channels = q_gate.shape
    modes = decay.shape[0]
    steps = tokens // SUB
    early = EARLY * (steps // CHUNKS)
    dma = pltpu.SemaphoreType.DMA
    state = (modes, channels)
    any_spec = pl.BlockSpec(memory_space=pl.ANY)
    vmem = pl.BlockSpec(memory_space=pltpu.VMEM)
    return pl.pallas_call(
        kernel,
        out_shape=jax.ShapeDtypeStruct((tokens, channels), BF16),
        in_specs=[any_spec] * 8,
        out_specs=vmem,
        scratch_shapes=[
            pltpu.VMEM(state, F32),
            pltpu.VMEM(state, F32),
            pltpu.VMEM((1, channels), F32),
            pltpu.VMEM((1, channels), F32),
            pltpu.VMEM((tokens, channels), BF16),
            pltpu.VMEM((tokens, channels), BF16),
            pltpu.VMEM((SUB, steps, channels), BF16),
            pltpu.VMEM(out_weight.shape, BF16),
            pltpu.VMEM((channels // LANES, tokens, LANES), F32),
            pltpu.VMEM((NY, channels // LANES, tokens, LANES), F32),
            pltpu.VMEM((steps, SUB, channels), F32),
            pltpu.VMEM((modes, SUB, channels), F32),
            pltpu.VMEM((NY,) + state, F32),
            pltpu.VMEM((NY, modes, SUB, channels), F32),
            pltpu.VMEM((NY, SUB, early, channels), BF16),
            pltpu.VMEM((NY, early * SUB, channels), BF16),
            pltpu.VMEM((NY,) + state, F32),
            pltpu.VMEM((NY,) + state, F32),
            pltpu.VMEM((modes, SUB, channels), F32),
            pltpu.VMEM((NZ,) + state, F32),
            pltpu.VMEM((NC, NX) + state, F32),
            pltpu.VMEM(state, F32),
            pltpu.VMEM(state, F32),
            pltpu.VMEM(state, F32),
            pltpu.VMEM(state, F32),
            pltpu.VMEM((NY, tokens, channels), BF16),
            pltpu.VMEM((channels // LANES, tokens, LANES), F32),
            dma((8,)), pltpu.SemaphoreType.REGULAR((NZ,)), pltpu.SemaphoreType.REGULAR((NX, NC)),
            dma((NZ,)), dma((NZ,)), dma((NX, NC)), dma((NC, NX)),
            dma((2,)), dma((2,)), dma((NY - 1, CHUNKS)), dma((NY, CHUNKS)),
        ]
        + [dma((count,)) for _ in range(4) for count in (NY - 1, NY)],
        compiler_params=pltpu.CompilerParams(
            collective_id=0, has_side_effects=True, vmem_limit_bytes=62 * 2**20
        ),
        name="layer",
    )(q_gate.reshape(SUB, steps, channels), k_gate, value, decay, residue, skip.reshape(1, -1), out_weight, out_bias.reshape(1, -1))


def solution(mesh):
    return jax.shard_map(
        layer,
        mesh=mesh,
        in_specs=(
            P("seq", "chan"),
            P("seq", "chan"),
            P("seq", "chan"),
            P(None, "chan"),
            P(None, "chan"),
            P("chan"),
            P(None, "chan"),
            P("chan"),
        ),
        out_specs=P("seq", "chan"),
        check_vma=False,
    )
```

```python
import functools

import jax
import jax.numpy as jnp
from jax import lax
from jax.experimental import pallas as pl
from jax.experimental.pallas import tpu as pltpu
from jax.sharding import PartitionSpec as P

MESH = pl.DeviceIdType.MESH
F32 = jnp.float32
BF16 = jnp.bfloat16
NX, NZ, NC, NY = 4, 8, 2, 4
SUB = 8
LANES = 128
CHUNKS = 8
LAG_EARLY, LEAD_EARLY = 4, 5


def tree(terms):
    while len(terms) > 1:
        terms = [a + b for a, b in zip(terms[::2], terms[1::2])] + terms[len(terms) // 2 * 2 :]
    return terms[0]


def rows_of(array, n, lane):
    return jnp.broadcast_to(array[n : n + 1, lane : lane + LANES], (SUB, LANES))


def kernel(
    q_hbm, k_hbm, v_hbm, decay_hbm, residue_hbm, skip_hbm, w_hbm, bias_hbm, out_ref,
    decay_ref, residue_ref, skip_ref, bias_ref, k_buf, v_buf, q_buf, w_buf,
    u_buf, qf_buf, y_buf, h_buf, lam_buf, sub_buf, g_buf,
    q_all, l_all, d_all, c_all, gathered, z_buf, x_buf, mate_s, mate_pre, t_buf, p_buf, o_buf,
    load_sem, mate_ready, y_ready, z_ready, x_ready, z_send, z_recv, x_send, x_recv, mate_send, mate_recv,
    late_send, late_recv, small_send, small_recv, ring_send, ring_recv,
):
    modes, channels = decay_ref.shape
    tokens = u_buf.shape[1]
    steps = tokens // SUB
    part = steps // CHUNKS
    lane_starts = range(0, channels, LANES)
    seq = lax.axis_index("seq")
    y = lax.axis_index("chan")
    x, z, core = seq // (NZ * NC), (seq // NC) % NZ, seq % NC
    half = NZ // 2
    lead = z < half
    following, previous, opposite = [(y + k) % NY for k in (1, 3, 2)]
    others = (following, previous, opposite)

    def device(xx, zz, cc, yy):
        return ((xx * NZ + zz) * NC + cc, yy)

    mate = device(x, z, 1 - core, y)

    def remote(src, dst, send, recv, where):
        return pltpu.make_async_remote_copy(
            src_ref=src, dst_ref=dst, send_sem=send, recv_sem=recv, device_id=where, device_id_type=MESH
        )

    def tell(semaphore, where):
        pl.semaphore_signal(semaphore, inc=1, device_id=where, device_id_type=MESH)

    loads = [
        pltpu.make_async_copy(src, dst, load_sem.at[i])
        for i, (src, dst) in enumerate(
            [
                (k_hbm, k_buf), (v_hbm, v_buf), (decay_hbm, decay_ref), (residue_hbm, residue_ref),
                (skip_hbm, skip_ref), (q_hbm, q_buf), (w_hbm, w_buf), (bias_hbm, bias_ref),
            ]
        )
    ]
    for load in loads:
        load.start()

    x_buf[...] = jnp.zeros_like(x_buf)
    z_buf[...] = jnp.zeros_like(z_buf)

    barrier = pltpu.get_barrier_semaphore()
    for k in range(1, NY):
        @pl.when(y + k < NY)
        def _(k=k):
            tell(barrier, device(x, z, core, y + k))

    @pl.when(core == 1)
    def _():
        tell(barrier, mate)

    for k in range(1, NZ):
        @pl.when(z + k < NZ)
        def _(k=k):
            tell(barrier, device(x, z + k, core, y))
    for k in range(1, NX):
        @pl.when(x + k < NX)
        def _(k=k):
            for cc in range(NC):
                tell(barrier, device(x + k, z, cc, y))
    earlier = 1 - core + y + z + NC * x

    @pl.when(earlier > 0)
    def _():
        pl.semaphore_wait(barrier, earlier)

    for k in range(1, NZ):
        @pl.when(z >= k)
        def _(k=k):
            tell(z_ready.at[z], device(x, z - k, core, y))
    for k in range(1, NX):
        @pl.when(x >= k)
        def _(k=k):
            for cc in range(NC):
                tell(x_ready.at[x, core], device(x - k, z, cc, y))
    for k in range(1, NY):
        @pl.when(y >= k)
        def _(k=k):
            tell(y_ready.at[y], device(x, z, core, y - k))

    @pl.when(core == 0)
    def _():
        tell(mate_ready, mate)

    spans = [(0, LAG_EARLY * part), (LAG_EARLY * part, LEAD_EARLY * part)]

    def rows(begin, end):
        return pl.ds(begin * SUB, (end - begin) * SUB)

    def hop(t, p, slot, which, target, i):
        begin, end = spans[p]
        size = (end - begin) * SUB // 2
        piece = (q_all, l_all)[t].at[slot, pl.ds(begin * SUB + which * size, size)]
        return remote(piece, piece, ring_send.at[t, p, i], ring_recv.at[t, p, slot, which], device(x, z, core, target))

    def own_hops(t, p):
        order = [(0, following), (1, previous), (1, following), (0, previous)]
        return [hop(t, p, y, which, target, i) for i, (which, target) in enumerate(order)]

    def forward_hops(t, p):
        return [hop(t, p, previous, 0, following, 4), hop(t, p, following, 1, previous, 5)]

    def ring_start(t, p):
        for copy in own_hops(t, p):
            copy.start()

    def ring_forward(t, p):
        for copy in forward_hops(t, p):
            copy.wait_recv()
            copy.start()

    def ring_finish(t, p):
        for slot, which in [(previous, 1), (following, 0), (opposite, 0), (opposite, 1)]:
            hop(t, p, slot, which, following, 0).wait_recv()

    def small_hops(t, buf, slot):
        return [
            remote(buf.at[slot], buf.at[slot], small_send.at[t, i], small_recv.at[t, slot], device(x, z, core, (y + k) % NY))
            for i, k in enumerate((2, 1, 3))
        ]

    def small_wait(t, buf, slot):
        remote(buf.at[slot], buf.at[slot], small_send.at[t, 0], small_recv.at[t, slot], mate).wait_recv()

    def late_hops(j):
        piece = gathered.at[y, rows(j * part, (j + 1) * part)]
        return [
            remote(piece, piece, late_send.at[i, j], late_recv.at[y, j], device(x, z, core, (y + k) % NY))
            for i, k in enumerate((2, 1, 3))
        ]

    def send_gate():
        loads[5].wait()
        for lane in lane_starts:
            qf_buf[lane // LANES] = q_buf[:, pl.ds(lane, LANES)].astype(F32)
        for lane in lane_starts:

            def spread(i, carry, lane=lane):
                pair = [qf_buf[lane // LANES, pl.ds(2 * i + o, SUB, stride=steps), :] for o in range(2)]
                start = pl.multiple_of(i * 2 * SUB, 2 * SUB)
                q_all[y, pl.ds(start, 2 * SUB), pl.ds(lane, LANES)] = jnp.concatenate(pair, axis=0).astype(BF16)
                return carry

            lax.fori_loop(0, steps // 2, spread, 0, unroll=8)
        ring_start(0, 0)

        @pl.when(lead)
        def _():
            ring_start(0, 1)

    loads[2].wait()
    decay = decay_ref[...]
    lam_buf[y] = jnp.exp(-decay)

    loads[0].wait()
    loads[1].wait()
    for lane in lane_starts:
        k_part, v_part = (buf[:, pl.ds(lane, LANES)].astype(F32) for buf in (k_buf, v_buf))
        u_buf[lane // LANES] = (k_part * v_part).astype(BF16).astype(F32)

    sublane = lax.broadcasted_iota(jnp.int32, (SUB, LANES), 0)
    for lane in lane_starts:
        lam = [rows_of(lam_buf[y], n, lane) for n in range(modes)]

        def advance(b, state, lam=lam, lane=lane):
            u = u_buf[lane // LANES, pl.ds(b, SUB, stride=steps), :]
            return tuple(l * h + u for l, h in zip(lam, state))

        zero = jnp.zeros((SUB, LANES), F32)
        state = lax.fori_loop(0, steps, advance, (zero,) * modes, unroll=8)
        for n in range(modes):
            run = state[n]
            for shift in (1, 2, 4):
                factor = jnp.exp(-rows_of(decay, n, lane) * float(steps * shift))
                moved = jnp.where(sublane >= shift, pltpu.roll(run, shift, 0), 0.0)
                run = run + factor * moved
            z_buf[pl.ds(z, 1), pl.ds(n, 1), pl.ds(lane, LANES)] = run[SUB - 1 : SUB].reshape(1, 1, LANES)
            h_buf[n, :, pl.ds(lane, LANES)] = jnp.where(sublane >= 1, pltpu.roll(run, 1, 0), 0.0)

    def state_copy(slot, target):
        return remote(z_buf.at[slot], z_buf.at[slot], z_send.at[target], z_recv.at[slot], device(x, target, core, y))

    def send_forward(k):
        pl.semaphore_wait(z_ready.at[z + k], 1)
        state_copy(z, z + k).start()

    needs_total = x < NX - 1
    s_copy = remote(z_buf.at[z], mate_s, mate_send.at[0], mate_recv.at[0], mate)
    for k in (4, 3, 5, 2, 6, 1, 7):
        @pl.when((z >= k) & needs_total)
        def _(k=k):
            state_copy(z, z - k).start()
    for k in range(1, half):
        @pl.when(~lead & (z + k < NZ))
        def _(k=k):
            send_forward(k)

    @pl.when(core == 1)
    def _():
        pl.semaphore_wait(mate_ready, 1)

    s_copy.start()
    for k in range(1, NY):
        @pl.when(y + k < NY)
        def _(k=k):
            pl.semaphore_wait(y_ready.at[y + k], 1)
    send_gate()

    d_all[y] = decay
    for copy in small_hops(0, d_all, y):
        copy.start()

    loads[3].wait()
    loads[4].wait()
    for begin, end in [spans[0], (spans[0][1], steps)]:
        for lane in lane_starts:
            lam = [rows_of(lam_buf[y], n, lane) for n in range(modes)]
            weight = [rows_of(residue_ref[...], n, lane) for n in range(modes)]
            skip_row = jnp.broadcast_to(skip_ref[:, lane : lane + LANES], (SUB, LANES))

            def local(i, state, lam=lam, weight=weight, skip_row=skip_row, lane=lane):
                pair = []
                for o in range(2):
                    b = 2 * i + o
                    u = u_buf[lane // LANES, pl.ds(b, SUB, stride=steps), :]
                    state = tuple(l * h + u for l, h in zip(lam, state))
                    total = tree([w * h for w, h in zip(weight, state)] + [skip_row * u])
                    y_buf[b, :, pl.ds(lane, LANES)] = total
                    pair.append(total)
                start = pl.multiple_of(i * 2 * SUB, 2 * SUB)
                l_all[y, pl.ds(start, 2 * SUB), pl.ds(lane, LANES)] = jnp.concatenate(pair, axis=0).astype(BF16)
                return state

            first = tuple(h_buf[n, :, pl.ds(lane, LANES)] for n in range(modes))
            last = lax.fori_loop(begin // 2, end // 2, local, first, unroll=2)
            for n in range(modes):
                h_buf[n, :, pl.ds(lane, LANES)] = last[n]
        if begin == 0:
            ring_start(1, 0)

    @pl.when(lead)
    def _():
        ring_start(1, 1)

    for k in range(1, NZ):
        @pl.when(lead & (z + k < NZ))
        def _(k=k):
            send_forward(k)

    @pl.when(lead)
    def _():
        ring_forward(0, 0)
        ring_forward(0, 1)


    place = (sublane * steps + 1).astype(F32)
    for lane in lane_starts:
        for n in range(modes):
            sub_buf[y, n, :, pl.ds(lane, LANES)] = jnp.exp(-rows_of(decay, n, lane) * place)
    chip_power = jnp.exp(-decay * float(NC * tokens))
    row_power = jnp.exp(-decay * float(NZ * NC * tokens))
    half_power = jnp.exp(-decay * float(tokens))
    place_power = jnp.exp(-decay * (z * (NC * tokens)).astype(F32))

    for k in range(1, NZ):
        @pl.when(z >= k)
        def _(k=k):
            state_copy(z - k, z).wait_recv()

        @pl.when((z + k < NZ) & needs_total)
        def _(k=k):
            state_copy(z + k, z).wait_recv()
    total = jnp.zeros_like(decay)
    prefix = jnp.zeros_like(decay)
    for zz in range(NZ):
        prefix = jnp.where(z == zz, total, prefix)
        total = chip_power * total + z_buf[zz]
    t_buf[...] = total
    p_buf[...] = prefix

    def total_copy(slot, target, cc):
        return remote(t_buf, x_buf.at[core, slot], x_send.at[target, cc], x_recv.at[core, slot], device(target, z, cc, y))

    for k in range(1, NX):
        @pl.when(x + k < NX)
        def _(k=k):
            for cc in range(NC):
                pl.semaphore_wait(x_ready.at[x + k, cc], 1)
                total_copy(x, x + k, cc).start()
    p_copy = remote(p_buf, mate_pre, mate_send.at[1], mate_recv.at[1], mate)
    p_copy.start()

    @pl.when(~lead)
    def _():
        ring_forward(0, 0)

    ring_forward(1, 0)

    @pl.when(lead)
    def _():
        ring_forward(1, 1)

    for src in others:
        small_wait(0, d_all, src)
        lam_buf[src] = jnp.exp(-d_all[src])
        for lane in lane_starts:
            for n in range(modes):
                sub_buf[src, n, :, pl.ds(lane, LANES)] = jnp.exp(-rows_of(d_all[src], n, lane) * place)
    s_copy.wait()
    p_copy.wait()
    for k in range(1, NX):
        @pl.when(x >= k)
        def _(k=k):
            for cc in range(NC):
                remote(t_buf, x_buf.at[cc, x - k], x_send.at[0, 0], x_recv.at[cc, x - k], mate).wait_recv()

    before = jnp.zeros_like(decay)
    for xx in range(NX - 1):
        step = half_power * x_buf[0, xx] + x_buf[1, xx]
        before = jnp.where(xx < x, row_power * before + step, before)
    other = mate_pre[...]
    first_core = jnp.where(core == 0, prefix, other)
    second_core = jnp.where(core == 0, other, prefix)
    carry = place_power * before + half_power * first_core + second_core
    carry = jnp.where(core == 0, carry, half_power * carry + mate_s[...])
    c_all[y] = residue_ref[...] * carry
    for copy in small_hops(1, c_all, y):
        copy.start()

    def start_carry(src, ahead=None):
        for lane in lane_starts:
            for n in range(modes):
                first = sub_buf[src, n, :, pl.ds(lane, LANES)] * rows_of(c_all[src], n, lane)
                if ahead is not None:
                    first = first * rows_of(ahead, n, lane)
                g_buf[n, :, pl.ds(lane, LANES)] = first

    def finish(src, begin, end, own):
        for lane in lane_starts:
            lam = [rows_of(lam_buf[src], n, lane) for n in range(modes)]

            def step(i, state, lam=lam, lane=lane):
                here = pl.ds(pl.multiple_of(i * 2 * SUB, 2 * SUB), 2 * SUB)
                gate = q_all[src, here, pl.ds(lane, LANES)].astype(F32)
                if own:
                    local = [y_buf[2 * i + o, :, pl.ds(lane, LANES)] for o in range(2)]
                else:
                    both = l_all[src, here, pl.ds(lane, LANES)].astype(F32)
                    local = [both[:SUB], both[SUB:]]
                pair = []
                for o in range(2):
                    pair.append(tree(list(state) + [local[o]]))
                    state = tuple(l * h for l, h in zip(lam, state))
                gathered[src, here, pl.ds(lane, LANES)] = (gate * jnp.concatenate(pair, axis=0)).astype(BF16)
                return state

            first = tuple(g_buf[n, :, pl.ds(lane, LANES)] for n in range(modes))
            last = lax.fori_loop(begin // 2, end // 2, step, first, unroll=4)
            for n in range(modes):
                g_buf[n, :, pl.ds(lane, LANES)] = last[n]

    def project(begin, end):
        projected = jnp.broadcast_to(bias_ref[...], ((end - begin) * SUB, channels))
        for yy in range(NY):
            projected = projected + jnp.dot(
                gathered[yy, rows(begin, end), :], w_buf[pl.ds(yy * channels, channels), :], preferred_element_type=F32
            )
        for i in range(end - begin):
            for lane in lane_starts:
                o_buf[lane // LANES, pl.ds(begin + i, SUB, stride=steps), :] = projected[
                    i * SUB : (i + 1) * SUB, lane : lane + LANES
                ]

    def late(first_late):
        for j in range(first_late, CHUNKS):
            finish(y, j * part, (j + 1) * part, True)
            for copy in late_hops(j):
                copy.start()

    start_carry(y, jnp.exp(-decay * jnp.where(lead, spans[1][1], spans[0][1]).astype(F32)))

    @pl.when(lead)
    def _():
        late(LEAD_EARLY)

    @pl.when(~lead)
    def _():
        late(LAG_EARLY)

    start_carry(y)
    finish(y, *spans[0], True)

    @pl.when(lead)
    def _():
        finish(y, *spans[1], True)

    for t in range(2):
        ring_finish(t, 0)

    @pl.when(lead)
    def _():
        for t in range(2):
            ring_finish(t, 1)

    for src in others:
        small_wait(1, c_all, src)
        start_carry(src)
        finish(src, *spans[0], False)

        @pl.when(lead)
        def _(src=src):
            finish(src, *spans[1], False)

    loads[6].wait()
    loads[7].wait()
    project(*spans[0])

    @pl.when(lead)
    def _():
        project(*spans[1])

    def project_late(first_late):
        for j in range(first_late, CHUNKS, 2):
            end = min(j + 2, CHUNKS)
            for i in range(j, end):
                for src in others:
                    piece = gathered.at[src, rows(i * part, (i + 1) * part)]
                    remote(piece, piece, late_send.at[0, i], late_recv.at[src, i], mate).wait_recv()
            project(j * part, end * part)

    @pl.when(lead)
    def _():
        project_late(LEAD_EARLY)

    @pl.when(~lead)
    def _():
        project_late(LAG_EARLY)

    for lane in lane_starts:
        out_ref[:, pl.ds(lane, LANES)] = o_buf[lane // LANES].astype(BF16)

    def sent(copies):
        for copy in copies:
            copy.wait_send()

    sent(small_hops(0, d_all, y) + small_hops(1, c_all, y))
    for t in range(2):
        sent(own_hops(t, 0) + forward_hops(t, 0))
    for j in range(LEAD_EARLY, CHUNKS):
        sent(late_hops(j))

    @pl.when(lead)
    def _():
        for t in range(2):
            sent(own_hops(t, 1) + forward_hops(t, 1))

    @pl.when(~lead)
    def _():
        for j in range(LAG_EARLY, LEAD_EARLY):
            sent(late_hops(j))

    for k in range(1, NZ):
        @pl.when(z + k < NZ)
        def _(k=k):
            state_copy(z, z + k).wait_send()

        @pl.when((z >= k) & needs_total)
        def _(k=k):
            state_copy(z, z - k).wait_send()
    for k in range(1, NX):
        @pl.when(x + k < NX)
        def _(k=k):
            for cc in range(NC):
                total_copy(x, x + k, cc).wait_send()


def layer(q_gate, k_gate, value, decay, residue, skip, out_weight, out_bias):
    tokens, channels = q_gate.shape
    modes = decay.shape[0]
    steps = tokens // SUB
    dma = pltpu.SemaphoreType.DMA
    regular = pltpu.SemaphoreType.REGULAR
    state = (modes, channels)
    by_lane = (channels // LANES, tokens, LANES)
    by_sublane = (modes, SUB, channels)
    any_spec = pl.BlockSpec(memory_space=pl.ANY)
    shapes = [
        (state, F32), (state, F32), ((1, channels), F32), ((1, channels), F32),
        ((tokens, channels), BF16), ((tokens, channels), BF16), ((tokens, channels), BF16),
        (out_weight.shape, BF16), (by_lane, F32), (by_lane, F32),
        ((steps, SUB, channels), F32), (by_sublane, F32),
        ((NY,) + state, F32), ((NY,) + by_sublane, F32), (by_sublane, F32),
        ((NY, tokens, channels), BF16), ((NY, tokens, channels), BF16),
        ((NY,) + state, F32), ((NY,) + state, F32),
        ((NY, tokens, channels), BF16),
        ((NZ,) + state, F32), ((NC, NX) + state, F32),
        (state, F32), (state, F32), (state, F32), (state, F32),
        (by_lane, F32),
    ]
    return pl.pallas_call(
        kernel,
        out_shape=jax.ShapeDtypeStruct((tokens, channels), BF16),
        in_specs=[any_spec] * 8,
        out_specs=pl.BlockSpec(memory_space=pltpu.VMEM),
        scratch_shapes=[pltpu.VMEM(*shape) for shape in shapes]
        + [
            dma((8,)), regular, regular((NY,)), regular((NZ,)), regular((NX, NC)), dma((NZ,)), dma((NZ,)), dma((NX, NC)), dma((NC, NX)),
            dma((2,)), dma((2,)), dma((NY - 1, CHUNKS)), dma((NY, CHUNKS)),
            dma((2, NY - 1)), dma((2, NY)), dma((2, 2, 6)), dma((2, 2, NY, 2)),
        ],
        compiler_params=pltpu.CompilerParams(
            collective_id=0, has_side_effects=True, vmem_limit_bytes=62 * 2**20
        ),
        name="layer",
    )(q_gate, k_gate, value, decay, residue, skip.reshape(1, -1), out_weight, out_bias.reshape(1, -1))


def solution(mesh):
    return jax.shard_map(
        layer,
        mesh=mesh,
        in_specs=(
            P("seq", "chan"),
            P("seq", "chan"),
            P("seq", "chan"),
            P(None, "chan"),
            P(None, "chan"),
            P("chan"),
            P(None, "chan"),
            P("chan"),
        ),
        out_specs=P("seq", "chan"),
        check_vma=False,
    )
```

```python
import functools

import jax
import jax.numpy as jnp
from jax import lax
from jax.experimental import pallas as pl
from jax.experimental.pallas import tpu as pltpu
from jax.sharding import PartitionSpec as P

MESH = pl.DeviceIdType.MESH
F32 = jnp.float32
BF16 = jnp.bfloat16
NX, NZ, NC, NY = 4, 8, 2, 4
SUB = 8
LANES = 128
CHUNKS = 8
LAG_EARLY, LEAD_EARLY = 4, 5


def tree(terms):
    while len(terms) > 1:
        terms = [a + b for a, b in zip(terms[::2], terms[1::2])] + terms[len(terms) // 2 * 2 :]
    return terms[0]


def rows_of(array, n, lane):
    return jnp.broadcast_to(array[n : n + 1, lane : lane + LANES], (SUB, LANES))


def kernel(
    q_hbm, k_hbm, v_hbm, decay_hbm, residue_hbm, skip_hbm, w_hbm, bias_hbm, out_ref,
    decay_ref, residue_ref, skip_ref, bias_ref, k_buf, v_buf, q_buf, w_buf,
    u_buf, qf_buf, y_buf, h_buf, lam_buf, sub_buf, g_buf,
    q_all, l_all, d_all, c_all, gathered, z_buf, x_buf, mate_s, mate_pre, t_buf, p_buf, o_buf,
    load_sem, mate_ready, y_ready, z_ready, x_ready, z_send, z_recv, x_send, x_recv, mate_send, mate_recv,
    late_send, late_recv, small_send, small_recv, ring_send, ring_recv,
):
    modes, channels = decay_ref.shape
    tokens = u_buf.shape[1]
    steps = tokens // SUB
    part = steps // CHUNKS
    lane_starts = range(0, channels, LANES)
    seq = lax.axis_index("seq")
    y = lax.axis_index("chan")
    x, z, core = seq // (NZ * NC), (seq // NC) % NZ, seq % NC
    half = NZ // 2
    lead = z < half
    following, previous, opposite = [(y + k) % NY for k in (1, 3, 2)]
    others = (following, previous, opposite)

    def device(xx, zz, cc, yy):
        return ((xx * NZ + zz) * NC + cc, yy)

    mate = device(x, z, 1 - core, y)

    def remote(src, dst, send, recv, where):
        return pltpu.make_async_remote_copy(
            src_ref=src, dst_ref=dst, send_sem=send, recv_sem=recv, device_id=where, device_id_type=MESH
        )

    def tell(semaphore, where):
        pl.semaphore_signal(semaphore, inc=1, device_id=where, device_id_type=MESH)

    loads = [
        pltpu.make_async_copy(src, dst, load_sem.at[i])
        for i, (src, dst) in enumerate(
            [
                (k_hbm, k_buf), (v_hbm, v_buf), (decay_hbm, decay_ref), (residue_hbm, residue_ref),
                (skip_hbm, skip_ref), (q_hbm, q_buf), (w_hbm, w_buf), (bias_hbm, bias_ref),
            ]
        )
    ]
    for load in loads:
        load.start()

    x_buf[...] = jnp.zeros_like(x_buf)
    z_buf[...] = jnp.zeros_like(z_buf)

    barrier = pltpu.get_barrier_semaphore()
    for k in range(1, NY):
        @pl.when(y + k < NY)
        def _(k=k):
            tell(barrier, device(x, z, core, y + k))

    @pl.when(core == 1)
    def _():
        tell(barrier, mate)

    for k in range(1, NZ):
        @pl.when(z + k < NZ)
        def _(k=k):
            tell(barrier, device(x, z + k, core, y))
    for k in range(1, NX):
        @pl.when(x + k < NX)
        def _(k=k):
            for cc in range(NC):
                tell(barrier, device(x + k, z, cc, y))
    earlier = 1 - core + y + z + NC * x

    @pl.when(earlier > 0)
    def _():
        pl.semaphore_wait(barrier, earlier)

    for k in range(1, NZ):
        @pl.when(z >= k)
        def _(k=k):
            tell(z_ready.at[z], device(x, z - k, core, y))
    for k in range(1, NX):
        @pl.when(x >= k)
        def _(k=k):
            for cc in range(NC):
                tell(x_ready.at[x, core], device(x - k, z, cc, y))
    for k in range(1, NY):
        @pl.when(y >= k)
        def _(k=k):
            tell(y_ready.at[y], device(x, z, core, y - k))

    @pl.when(core == 0)
    def _():
        tell(mate_ready, mate)

    spans = [(0, LAG_EARLY * part), (LAG_EARLY * part, LEAD_EARLY * part)]

    def rows(begin, end):
        return pl.ds(begin * SUB, (end - begin) * SUB)

    def hop(t, p, slot, which, target, i):
        begin, end = spans[p]
        size = (end - begin) * SUB // 2
        piece = (q_all, l_all)[t].at[slot, pl.ds(begin * SUB + which * size, size)]
        return remote(piece, piece, ring_send.at[t, p, i], ring_recv.at[t, p, slot, which], device(x, z, core, target))

    def own_hops(t, p):
        order = [(0, following), (1, previous), (1, following), (0, previous)]
        return [hop(t, p, y, which, target, i) for i, (which, target) in enumerate(order)]

    def forward_hops(t, p):
        return [hop(t, p, previous, 0, following, 4), hop(t, p, following, 1, previous, 5)]

    def ring_start(t, p):
        for copy in own_hops(t, p):
            copy.start()

    def ring_forward(t, p):
        for copy in forward_hops(t, p):
            copy.wait_recv()
            copy.start()

    def ring_finish(t, p):
        for slot, which in [(previous, 1), (following, 0), (opposite, 0), (opposite, 1)]:
            hop(t, p, slot, which, following, 0).wait_recv()

    def small_hops(t, buf, slot):
        return [
            remote(buf.at[slot], buf.at[slot], small_send.at[t, i], small_recv.at[t, slot], device(x, z, core, (y + k) % NY))
            for i, k in enumerate((2, 1, 3))
        ]

    def small_wait(t, buf, slot):
        remote(buf.at[slot], buf.at[slot], small_send.at[t, 0], small_recv.at[t, slot], mate).wait_recv()

    def late_hops(j):
        piece = gathered.at[y, rows(j * part, (j + 1) * part)]
        return [
            remote(piece, piece, late_send.at[i, j], late_recv.at[y, j], device(x, z, core, (y + k) % NY))
            for i, k in enumerate((2, 1, 3))
        ]

    def send_gate():
        loads[5].wait()
        for lane in lane_starts:
            qf_buf[lane // LANES] = q_buf[:, pl.ds(lane, LANES)].astype(F32)
        for lane in lane_starts:

            def spread(i, carry, lane=lane):
                pair = [qf_buf[lane // LANES, pl.ds(2 * i + o, SUB, stride=steps), :] for o in range(2)]
                start = pl.multiple_of(i * 2 * SUB, 2 * SUB)
                q_all[y, pl.ds(start, 2 * SUB), pl.ds(lane, LANES)] = jnp.concatenate(pair, axis=0).astype(BF16)
                return carry

            lax.fori_loop(0, steps // 2, spread, 0, unroll=8)
        ring_start(0, 0)

        @pl.when(lead)
        def _():
            ring_start(0, 1)

    loads[2].wait()
    decay = decay_ref[...]
    lam_buf[y] = jnp.exp(-decay)

    scan_power = {shift: jnp.exp(-decay * float(steps * shift)) for shift in (1, 2, 4)}

    loads[0].wait()
    loads[1].wait()
    for lane in lane_starts:
        k_part, v_part = (buf[:, pl.ds(lane, LANES)].astype(F32) for buf in (k_buf, v_buf))
        u_buf[lane // LANES] = (k_part * v_part).astype(BF16).astype(F32)

    sublane = lax.broadcasted_iota(jnp.int32, (SUB, LANES), 0)
    for lane in lane_starts:
        lam = [rows_of(lam_buf[y], n, lane) for n in range(modes)]

        def advance(b, state, lam=lam, lane=lane):
            u = u_buf[lane // LANES, pl.ds(b, SUB, stride=steps), :]
            return tuple(l * h + u for l, h in zip(lam, state))

        zero = jnp.zeros((SUB, LANES), F32)
        state = lax.fori_loop(0, steps, advance, (zero,) * modes, unroll=8)
        for n in range(modes):
            run = state[n]
            for shift in (1, 2, 4):
                factor = rows_of(scan_power[shift], n, lane)
                moved = jnp.where(sublane >= shift, pltpu.roll(run, shift, 0), 0.0)
                run = run + factor * moved
            z_buf[pl.ds(z, 1), pl.ds(n, 1), pl.ds(lane, LANES)] = run[SUB - 1 : SUB].reshape(1, 1, LANES)
            h_buf[n, :, pl.ds(lane, LANES)] = jnp.where(sublane >= 1, pltpu.roll(run, 1, 0), 0.0)

    def state_copy(slot, target):
        return remote(z_buf.at[slot], z_buf.at[slot], z_send.at[target], z_recv.at[slot], device(x, target, core, y))

    def send_forward(k):
        pl.semaphore_wait(z_ready.at[z + k], 1)
        state_copy(z, z + k).start()

    needs_total = x < NX - 1
    s_copy = remote(z_buf.at[z], mate_s, mate_send.at[0], mate_recv.at[0], mate)
    for k in (4, 3, 5, 2, 6, 1, 7):
        @pl.when((z >= k) & needs_total)
        def _(k=k):
            state_copy(z, z - k).start()
    for k in range(1, half):
        @pl.when(~lead & (z + k < NZ))
        def _(k=k):
            send_forward(k)

    @pl.when(core == 1)
    def _():
        pl.semaphore_wait(mate_ready, 1)

    s_copy.start()
    for k in range(1, NY):
        @pl.when(y + k < NY)
        def _(k=k):
            pl.semaphore_wait(y_ready.at[y + k], 1)
    send_gate()

    d_all[y] = decay
    for copy in small_hops(0, d_all, y):
        copy.start()

    loads[3].wait()
    loads[4].wait()
    for begin, end in [spans[0], (spans[0][1], steps)]:
        for lane in lane_starts:
            lam = [rows_of(lam_buf[y], n, lane) for n in range(modes)]
            weight = [rows_of(residue_ref[...], n, lane) for n in range(modes)]
            skip_row = jnp.broadcast_to(skip_ref[:, lane : lane + LANES], (SUB, LANES))

            def local(i, state, lam=lam, weight=weight, skip_row=skip_row, lane=lane):
                pair = []
                for o in range(2):
                    b = 2 * i + o
                    u = u_buf[lane // LANES, pl.ds(b, SUB, stride=steps), :]
                    state = tuple(l * h + u for l, h in zip(lam, state))
                    total = tree([w * h for w, h in zip(weight, state)] + [skip_row * u])
                    y_buf[b, :, pl.ds(lane, LANES)] = total
                    pair.append(total)
                start = pl.multiple_of(i * 2 * SUB, 2 * SUB)
                l_all[y, pl.ds(start, 2 * SUB), pl.ds(lane, LANES)] = jnp.concatenate(pair, axis=0).astype(BF16)
                return state

            first = tuple(h_buf[n, :, pl.ds(lane, LANES)] for n in range(modes))
            last = lax.fori_loop(begin // 2, end // 2, local, first, unroll=2)
            for n in range(modes):
                h_buf[n, :, pl.ds(lane, LANES)] = last[n]
        if begin == 0:
            ring_start(1, 0)

    @pl.when(lead)
    def _():
        ring_start(1, 1)

    for k in range(1, NZ):
        @pl.when(lead & (z + k < NZ))
        def _(k=k):
            send_forward(k)

    @pl.when(lead)
    def _():
        ring_forward(0, 0)
        ring_forward(0, 1)


    place = (sublane * steps + 1).astype(F32)
    for lane in lane_starts:
        for n in range(modes):
            sub_buf[y, n, :, pl.ds(lane, LANES)] = jnp.exp(-rows_of(decay, n, lane) * place)
    chip_power = jnp.exp(-decay * float(NC * tokens))
    row_power = jnp.exp(-decay * float(NZ * NC * tokens))
    half_power = jnp.exp(-decay * float(tokens))
    place_power = jnp.exp(-decay * (z * (NC * tokens)).astype(F32))

    for k in range(1, NZ):
        @pl.when(z >= k)
        def _(k=k):
            state_copy(z - k, z).wait_recv()

        @pl.when((z + k < NZ) & needs_total)
        def _(k=k):
            state_copy(z + k, z).wait_recv()
    total = jnp.zeros_like(decay)
    prefix = jnp.zeros_like(decay)
    for zz in range(NZ):
        prefix = jnp.where(z == zz, total, prefix)
        total = chip_power * total + z_buf[zz]
    t_buf[...] = total
    p_buf[...] = prefix

    def total_copy(slot, target, cc):
        return remote(t_buf, x_buf.at[core, slot], x_send.at[target, cc], x_recv.at[core, slot], device(target, z, cc, y))

    for k in range(1, NX):
        @pl.when(x + k < NX)
        def _(k=k):
            for cc in range(NC):
                pl.semaphore_wait(x_ready.at[x + k, cc], 1)
                total_copy(x, x + k, cc).start()
    p_copy = remote(p_buf, mate_pre, mate_send.at[1], mate_recv.at[1], mate)
    p_copy.start()

    @pl.when(~lead)
    def _():
        ring_forward(0, 0)

    ring_forward(1, 0)

    @pl.when(lead)
    def _():
        ring_forward(1, 1)

    for src in others:
        small_wait(0, d_all, src)
        lam_buf[src] = jnp.exp(-d_all[src])
        for lane in lane_starts:
            for n in range(modes):
                sub_buf[src, n, :, pl.ds(lane, LANES)] = jnp.exp(-rows_of(d_all[src], n, lane) * place)
    s_copy.wait()
    p_copy.wait()
    for k in range(1, NX):
        @pl.when(x >= k)
        def _(k=k):
            for cc in range(NC):
                remote(t_buf, x_buf.at[cc, x - k], x_send.at[0, 0], x_recv.at[cc, x - k], mate).wait_recv()

    before = jnp.zeros_like(decay)
    for xx in range(NX - 1):
        step = half_power * x_buf[0, xx] + x_buf[1, xx]
        before = jnp.where(xx < x, row_power * before + step, before)
    other = mate_pre[...]
    first_core = jnp.where(core == 0, prefix, other)
    second_core = jnp.where(core == 0, other, prefix)
    carry = place_power * before + half_power * first_core + second_core
    carry = jnp.where(core == 0, carry, half_power * carry + mate_s[...])
    c_all[y] = residue_ref[...] * carry
    for copy in small_hops(1, c_all, y):
        copy.start()

    def start_carry(src, ahead=None):
        for lane in lane_starts:
            for n in range(modes):
                first = sub_buf[src, n, :, pl.ds(lane, LANES)] * rows_of(c_all[src], n, lane)
                if ahead is not None:
                    first = first * rows_of(ahead, n, lane)
                g_buf[n, :, pl.ds(lane, LANES)] = first

    def finish(src, begin, end, own):
        for lane in lane_starts:
            lam = [rows_of(lam_buf[src], n, lane) for n in range(modes)]

            def step(i, state, lam=lam, lane=lane):
                here = pl.ds(pl.multiple_of(i * 2 * SUB, 2 * SUB), 2 * SUB)
                gate = q_all[src, here, pl.ds(lane, LANES)].astype(F32)
                if own:
                    local = [y_buf[2 * i + o, :, pl.ds(lane, LANES)] for o in range(2)]
                else:
                    both = l_all[src, here, pl.ds(lane, LANES)].astype(F32)
                    local = [both[:SUB], both[SUB:]]
                pair = []
                for o in range(2):
                    pair.append(tree(list(state) + [local[o]]))
                    state = tuple(l * h for l, h in zip(lam, state))
                gathered[src, here, pl.ds(lane, LANES)] = (gate * jnp.concatenate(pair, axis=0)).astype(BF16)
                return state

            first = tuple(g_buf[n, :, pl.ds(lane, LANES)] for n in range(modes))
            last = lax.fori_loop(begin // 2, end // 2, step, first, unroll=4)
            for n in range(modes):
                g_buf[n, :, pl.ds(lane, LANES)] = last[n]

    def project(begin, end):
        projected = jnp.broadcast_to(bias_ref[...], ((end - begin) * SUB, channels))
        for yy in range(NY):
            projected = projected + jnp.dot(
                gathered[yy, rows(begin, end), :], w_buf[pl.ds(yy * channels, channels), :], preferred_element_type=F32
            )
        for i in range(end - begin):
            for lane in lane_starts:
                o_buf[lane // LANES, pl.ds(begin + i, SUB, stride=steps), :] = projected[
                    i * SUB : (i + 1) * SUB, lane : lane + LANES
                ]

    def late(first_late):
        for j in range(first_late, CHUNKS):
            finish(y, j * part, (j + 1) * part, True)
            for copy in late_hops(j):
                copy.start()

    start_carry(y, jnp.exp(-decay * jnp.where(lead, spans[1][1], spans[0][1]).astype(F32)))

    @pl.when(lead)
    def _():
        late(LEAD_EARLY)

    @pl.when(~lead)
    def _():
        late(LAG_EARLY)

    start_carry(y)
    finish(y, *spans[0], True)

    @pl.when(lead)
    def _():
        finish(y, *spans[1], True)

    for t in range(2):
        ring_finish(t, 0)

    @pl.when(lead)
    def _():
        for t in range(2):
            ring_finish(t, 1)

    for src in others:
        small_wait(1, c_all, src)
        start_carry(src)
        finish(src, *spans[0], False)

        @pl.when(lead)
        def _(src=src):
            finish(src, *spans[1], False)

    loads[6].wait()
    loads[7].wait()
    project(*spans[0])

    @pl.when(lead)
    def _():
        project(*spans[1])

    def project_late(first_late):
        for j in range(first_late, CHUNKS, 2):
            end = min(j + 2, CHUNKS)
            for i in range(j, end):
                for src in others:
                    piece = gathered.at[src, rows(i * part, (i + 1) * part)]
                    remote(piece, piece, late_send.at[0, i], late_recv.at[src, i], mate).wait_recv()
            project(j * part, end * part)

    @pl.when(lead)
    def _():
        project_late(LEAD_EARLY)

    @pl.when(~lead)
    def _():
        project_late(LAG_EARLY)

    for lane in lane_starts:
        out_ref[:, pl.ds(lane, LANES)] = o_buf[lane // LANES].astype(BF16)

    def sent(copies):
        for copy in copies:
            copy.wait_send()

    sent(small_hops(0, d_all, y) + small_hops(1, c_all, y))
    for t in range(2):
        sent(own_hops(t, 0) + forward_hops(t, 0))
    for j in range(LEAD_EARLY, CHUNKS):
        sent(late_hops(j))

    @pl.when(lead)
    def _():
        for t in range(2):
            sent(own_hops(t, 1) + forward_hops(t, 1))

    @pl.when(~lead)
    def _():
        for j in range(LAG_EARLY, LEAD_EARLY):
            sent(late_hops(j))

    for k in range(1, NZ):
        @pl.when(z + k < NZ)
        def _(k=k):
            state_copy(z, z + k).wait_send()

        @pl.when((z >= k) & needs_total)
        def _(k=k):
            state_copy(z, z - k).wait_send()
    for k in range(1, NX):
        @pl.when(x + k < NX)
        def _(k=k):
            for cc in range(NC):
                total_copy(x, x + k, cc).wait_send()


def layer(q_gate, k_gate, value, decay, residue, skip, out_weight, out_bias):
    tokens, channels = q_gate.shape
    modes = decay.shape[0]
    steps = tokens // SUB
    dma = pltpu.SemaphoreType.DMA
    regular = pltpu.SemaphoreType.REGULAR
    state = (modes, channels)
    by_lane = (channels // LANES, tokens, LANES)
    by_sublane = (modes, SUB, channels)
    any_spec = pl.BlockSpec(memory_space=pl.ANY)
    shapes = [
        (state, F32), (state, F32), ((1, channels), F32), ((1, channels), F32),
        ((tokens, channels), BF16), ((tokens, channels), BF16), ((tokens, channels), BF16),
        (out_weight.shape, BF16), (by_lane, F32), (by_lane, F32),
        ((steps, SUB, channels), F32), (by_sublane, F32),
        ((NY,) + state, F32), ((NY,) + by_sublane, F32), (by_sublane, F32),
        ((NY, tokens, channels), BF16), ((NY, tokens, channels), BF16),
        ((NY,) + state, F32), ((NY,) + state, F32),
        ((NY, tokens, channels), BF16),
        ((NZ,) + state, F32), ((NC, NX) + state, F32),
        (state, F32), (state, F32), (state, F32), (state, F32),
        (by_lane, F32),
    ]
    return pl.pallas_call(
        kernel,
        out_shape=pltpu.VMEM((tokens, channels), BF16),
        in_specs=[any_spec] * 8,
        out_specs=pl.BlockSpec(memory_space=pltpu.VMEM),
        scratch_shapes=[pltpu.VMEM(*shape) for shape in shapes]
        + [
            dma((8,)), regular, regular((NY,)), regular((NZ,)), regular((NX, NC)), dma((NZ,)), dma((NZ,)), dma((NX, NC)), dma((NC, NX)),
            dma((2,)), dma((2,)), dma((NY - 1, CHUNKS)), dma((NY, CHUNKS)),
            dma((2, NY - 1)), dma((2, NY)), dma((2, 2, 6)), dma((2, 2, NY, 2)),
        ],
        compiler_params=pltpu.CompilerParams(
            collective_id=0, has_side_effects=True, vmem_limit_bytes=62 * 2**20
        ),
        name="layer",
    )(q_gate, k_gate, value, decay, residue, skip.reshape(1, -1), out_weight, out_bias.reshape(1, -1))


def solution(mesh):
    return jax.shard_map(
        layer,
        mesh=mesh,
        in_specs=(
            P("seq", "chan"),
            P("seq", "chan"),
            P("seq", "chan"),
            P(None, "chan"),
            P(None, "chan"),
            P("chan"),
            P(None, "chan"),
            P("chan"),
        ),
        out_specs=P("seq", "chan"),
        check_vma=False,
    )
```

```python
import functools

import jax
import jax.numpy as jnp
from jax import lax
from jax.experimental import pallas as pl
from jax.experimental.pallas import tpu as pltpu
from jax.sharding import PartitionSpec as P

MESH = pl.DeviceIdType.MESH
F32 = jnp.float32
BF16 = jnp.bfloat16
NX, NZ, NC, NY = 4, 8, 2, 4
SUB = 8
LANES = 128
CHUNKS = 8
LAG_EARLY, LEAD_EARLY = 4, 5


def tree(terms):
    while len(terms) > 1:
        terms = [a + b for a, b in zip(terms[::2], terms[1::2])] + terms[len(terms) // 2 * 2 :]
    return terms[0]


def rows_of(array, n, lane):
    return jnp.broadcast_to(array[n : n + 1, lane : lane + LANES], (SUB, LANES))


def kernel(
    q_hbm, k_hbm, v_hbm, decay_hbm, residue_hbm, skip_hbm, w_hbm, bias_hbm, out_ref,
    decay_ref, residue_ref, skip_ref, bias_ref, k_buf, v_buf, q_buf, w_buf,
    u_buf, qf_buf, y_buf, h_buf, lam_buf, sub_buf, g_buf,
    q_all, l_all, d_all, c_all, gathered, z_buf, x_buf, mate_s, mate_pre, t_buf, p_buf, o_buf,
    load_sem, mate_ready, y_ready, z_ready, x_ready, z_send, z_recv, x_send, x_recv, mate_send, mate_recv,
    late_send, late_recv, small_send, small_recv, ring_send, ring_recv,
):
    modes, channels = decay_ref.shape
    tokens = u_buf.shape[1]
    steps = tokens // SUB
    part = steps // CHUNKS
    lane_starts = range(0, channels, LANES)
    seq = lax.axis_index("seq")
    y = lax.axis_index("chan")
    x, z, core = seq // (NZ * NC), (seq // NC) % NZ, seq % NC
    half = NZ // 2
    lead = z < half
    following, previous, opposite = [(y + k) % NY for k in (1, 3, 2)]
    others = (following, previous, opposite)

    def device(xx, zz, cc, yy):
        return ((xx * NZ + zz) * NC + cc, yy)

    mate = device(x, z, 1 - core, y)

    def remote(src, dst, send, recv, where):
        return pltpu.make_async_remote_copy(
            src_ref=src, dst_ref=dst, send_sem=send, recv_sem=recv, device_id=where, device_id_type=MESH
        )

    def tell(semaphore, where):
        pl.semaphore_signal(semaphore, inc=1, device_id=where, device_id_type=MESH)

    loads = [
        pltpu.make_async_copy(src, dst, load_sem.at[i])
        for i, (src, dst) in enumerate(
            [
                (k_hbm, k_buf), (v_hbm, v_buf), (decay_hbm, decay_ref), (residue_hbm, residue_ref),
                (skip_hbm, skip_ref), (q_hbm, q_buf), (w_hbm, w_buf), (bias_hbm, bias_ref),
            ]
        )
    ]
    for load in loads:
        load.start()

    x_buf[...] = jnp.zeros_like(x_buf)
    z_buf[...] = jnp.zeros_like(z_buf)

    barrier = pltpu.get_barrier_semaphore()
    for k in range(1, NY):
        @pl.when(y + k < NY)
        def _(k=k):
            tell(barrier, device(x, z, core, y + k))

    @pl.when(core == 1)
    def _():
        tell(barrier, mate)

    for k in range(1, NZ):
        @pl.when(z + k < NZ)
        def _(k=k):
            tell(barrier, device(x, z + k, core, y))
    for k in range(1, NX):
        @pl.when(x + k < NX)
        def _(k=k):
            for cc in range(NC):
                tell(barrier, device(x + k, z, cc, y))
    earlier = 1 - core + y + z + NC * x

    @pl.when(earlier > 0)
    def _():
        pl.semaphore_wait(barrier, earlier)

    for k in range(1, NZ):
        @pl.when(z >= k)
        def _(k=k):
            tell(z_ready.at[z], device(x, z - k, core, y))
    for k in range(1, NX):
        @pl.when(x >= k)
        def _(k=k):
            for cc in range(NC):
                tell(x_ready.at[x, core], device(x - k, z, cc, y))
    for k in range(1, NY):
        @pl.when(y >= k)
        def _(k=k):
            tell(y_ready.at[y], device(x, z, core, y - k))

    @pl.when(core == 0)
    def _():
        tell(mate_ready, mate)

    spans = [(0, LAG_EARLY * part), (LAG_EARLY * part, LEAD_EARLY * part)]

    def rows(begin, end):
        return pl.ds(begin * SUB, (end - begin) * SUB)

    def hop(t, p, slot, which, target, i):
        begin, end = spans[p]
        size = (end - begin) * SUB // 2
        piece = (q_all, l_all)[t].at[slot, pl.ds(begin * SUB + which * size, size)]
        return remote(piece, piece, ring_send.at[t, p, i], ring_recv.at[t, p, slot, which], device(x, z, core, target))

    def own_hops(t, p):
        order = [(0, following), (1, previous), (1, following), (0, previous)]
        return [hop(t, p, y, which, target, i) for i, (which, target) in enumerate(order)]

    def forward_hops(t, p):
        return [hop(t, p, previous, 0, following, 4), hop(t, p, following, 1, previous, 5)]

    def ring_start(t, p):
        for copy in own_hops(t, p):
            copy.start()

    def ring_forward(t, p):
        for copy in forward_hops(t, p):
            copy.wait_recv()
            copy.start()

    def ring_finish(t, p):
        for slot, which in [(previous, 1), (following, 0), (opposite, 0), (opposite, 1)]:
            hop(t, p, slot, which, following, 0).wait_recv()

    def small_hops(t, buf, slot):
        return [
            remote(buf.at[slot], buf.at[slot], small_send.at[t, i], small_recv.at[t, slot], device(x, z, core, (y + k) % NY))
            for i, k in enumerate((2, 1, 3))
        ]

    def small_wait(t, buf, slot):
        remote(buf.at[slot], buf.at[slot], small_send.at[t, 0], small_recv.at[t, slot], mate).wait_recv()

    def late_hops(j):
        piece = gathered.at[y, rows(j * part, (j + 1) * part)]
        return [
            remote(piece, piece, late_send.at[i, j], late_recv.at[y, j], device(x, z, core, (y + k) % NY))
            for i, k in enumerate((2, 1, 3))
        ]

    def send_gate():
        loads[5].wait()
        for lane in lane_starts:
            qf_buf[lane // LANES] = q_buf[:, pl.ds(lane, LANES)].astype(F32)
        for lane in lane_starts:

            def spread(i, carry, lane=lane):
                pair = [qf_buf[lane // LANES, pl.ds(2 * i + o, SUB, stride=steps), :] for o in range(2)]
                start = pl.multiple_of(i * 2 * SUB, 2 * SUB)
                q_all[y, pl.ds(start, 2 * SUB), pl.ds(lane, LANES)] = jnp.concatenate(pair, axis=0).astype(BF16)
                return carry

            lax.fori_loop(0, steps // 2, spread, 0, unroll=8)
        ring_start(0, 0)

        @pl.when(lead)
        def _():
            ring_start(0, 1)

    loads[2].wait()
    decay = decay_ref[...]
    lam_buf[y] = jnp.exp(-decay)

    scan_power = {shift: jnp.exp(-decay * float(steps * shift)) for shift in (1, 2, 4)}

    loads[0].wait()
    loads[1].wait()
    for lane in lane_starts:
        k_part, v_part = (buf[:, pl.ds(lane, LANES)].astype(F32) for buf in (k_buf, v_buf))
        u_buf[lane // LANES] = (k_part * v_part).astype(BF16).astype(F32)

    sublane = lax.broadcasted_iota(jnp.int32, (SUB, LANES), 0)
    for lane in lane_starts:
        lam = [rows_of(lam_buf[y], n, lane) for n in range(modes)]

        def advance(b, state, lam=lam, lane=lane):
            u = u_buf[lane // LANES, pl.ds(b, SUB, stride=steps), :]
            return tuple(l * h + u for l, h in zip(lam, state))

        zero = jnp.zeros((SUB, LANES), F32)
        state = lax.fori_loop(0, steps, advance, (zero,) * modes, unroll=8)
        for n in range(modes):
            run = state[n]
            for shift in (1, 2, 4):
                factor = rows_of(scan_power[shift], n, lane)
                moved = jnp.where(sublane >= shift, pltpu.roll(run, shift, 0), 0.0)
                run = run + factor * moved
            z_buf[pl.ds(z, 1), pl.ds(n, 1), pl.ds(lane, LANES)] = run[SUB - 1 : SUB].reshape(1, 1, LANES)
            h_buf[n, :, pl.ds(lane, LANES)] = jnp.where(sublane >= 1, pltpu.roll(run, 1, 0), 0.0)

    def state_copy(slot, target):
        return remote(z_buf.at[slot], z_buf.at[slot], z_send.at[target], z_recv.at[slot], device(x, target, core, y))

    def send_forward(k):
        pl.semaphore_wait(z_ready.at[z + k], 1)
        state_copy(z, z + k).start()

    needs_total = x < NX - 1
    s_copy = remote(z_buf.at[z], mate_s, mate_send.at[0], mate_recv.at[0], mate)
    for k in (4, 3, 5, 2, 6, 1, 7):
        @pl.when((z >= k) & needs_total)
        def _(k=k):
            state_copy(z, z - k).start()
    for k in range(1, half):
        @pl.when(~lead & (z + k < NZ))
        def _(k=k):
            send_forward(k)

    @pl.when(core == 1)
    def _():
        pl.semaphore_wait(mate_ready, 1)

    s_copy.start()
    for k in range(1, NY):
        @pl.when(y + k < NY)
        def _(k=k):
            pl.semaphore_wait(y_ready.at[y + k], 1)
    send_gate()

    d_all[y] = decay
    for copy in small_hops(0, d_all, y):
        copy.start()

    loads[3].wait()
    loads[4].wait()
    for begin, end in [spans[0], (spans[0][1], steps)]:
        for lane in lane_starts:
            lam = [rows_of(lam_buf[y], n, lane) for n in range(modes)]
            weight = [rows_of(residue_ref[...], n, lane) for n in range(modes)]
            skip_row = jnp.broadcast_to(skip_ref[:, lane : lane + LANES], (SUB, LANES))

            def local(i, state, lam=lam, weight=weight, skip_row=skip_row, lane=lane):
                pair = []
                for o in range(2):
                    b = 2 * i + o
                    u = u_buf[lane // LANES, pl.ds(b, SUB, stride=steps), :]
                    state = tuple(l * h + u for l, h in zip(lam, state))
                    total = tree([w * h for w, h in zip(weight, state)] + [skip_row * u])
                    y_buf[b, :, pl.ds(lane, LANES)] = total
                    pair.append(total)
                start = pl.multiple_of(i * 2 * SUB, 2 * SUB)
                l_all[y, pl.ds(start, 2 * SUB), pl.ds(lane, LANES)] = jnp.concatenate(pair, axis=0).astype(BF16)
                return state

            first = tuple(h_buf[n, :, pl.ds(lane, LANES)] for n in range(modes))
            last = lax.fori_loop(begin // 2, end // 2, local, first, unroll=2)
            for n in range(modes):
                h_buf[n, :, pl.ds(lane, LANES)] = last[n]
        if begin == 0:
            ring_start(1, 0)
            for k in range(1, NZ):
                @pl.when(lead & (z + k < NZ))
                def _(k=k):
                    send_forward(k)

    @pl.when(lead)
    def _():
        ring_start(1, 1)

    @pl.when(lead)
    def _():
        ring_forward(0, 0)
        ring_forward(0, 1)


    place = (sublane * steps + 1).astype(F32)
    for lane in lane_starts:
        for n in range(modes):
            sub_buf[y, n, :, pl.ds(lane, LANES)] = jnp.exp(-rows_of(decay, n, lane) * place)
    chip_power = jnp.exp(-decay * float(NC * tokens))
    row_power = jnp.exp(-decay * float(NZ * NC * tokens))
    half_power = jnp.exp(-decay * float(tokens))
    place_power = jnp.exp(-decay * (z * (NC * tokens)).astype(F32))

    for k in range(1, NZ):
        @pl.when(z >= k)
        def _(k=k):
            state_copy(z - k, z).wait_recv()

        @pl.when((z + k < NZ) & needs_total)
        def _(k=k):
            state_copy(z + k, z).wait_recv()
    total = jnp.zeros_like(decay)
    prefix = jnp.zeros_like(decay)
    for zz in range(NZ):
        prefix = jnp.where(z == zz, total, prefix)
        total = chip_power * total + z_buf[zz]
    t_buf[...] = total
    p_buf[...] = prefix

    def total_copy(slot, target, cc):
        return remote(t_buf, x_buf.at[core, slot], x_send.at[target, cc], x_recv.at[core, slot], device(target, z, cc, y))

    for k in range(1, NX):
        @pl.when(x + k < NX)
        def _(k=k):
            for cc in range(NC):
                pl.semaphore_wait(x_ready.at[x + k, cc], 1)
                total_copy(x, x + k, cc).start()
    p_copy = remote(p_buf, mate_pre, mate_send.at[1], mate_recv.at[1], mate)
    p_copy.start()

    @pl.when(~lead)
    def _():
        ring_forward(0, 0)

    ring_forward(1, 0)

    @pl.when(lead)
    def _():
        ring_forward(1, 1)

    for src in others:
        small_wait(0, d_all, src)
        lam_buf[src] = jnp.exp(-d_all[src])
        for lane in lane_starts:
            for n in range(modes):
                sub_buf[src, n, :, pl.ds(lane, LANES)] = jnp.exp(-rows_of(d_all[src], n, lane) * place)
    s_copy.wait()
    p_copy.wait()
    for k in range(1, NX):
        @pl.when(x >= k)
        def _(k=k):
            for cc in range(NC):
                remote(t_buf, x_buf.at[cc, x - k], x_send.at[0, 0], x_recv.at[cc, x - k], mate).wait_recv()

    before = jnp.zeros_like(decay)
    for xx in range(NX - 1):
        step = half_power * x_buf[0, xx] + x_buf[1, xx]
        before = jnp.where(xx < x, row_power * before + step, before)
    other = mate_pre[...]
    first_core = jnp.where(core == 0, prefix, other)
    second_core = jnp.where(core == 0, other, prefix)
    carry = place_power * before + half_power * first_core + second_core
    carry = jnp.where(core == 0, carry, half_power * carry + mate_s[...])
    c_all[y] = residue_ref[...] * carry
    for copy in small_hops(1, c_all, y):
        copy.start()

    def start_carry(src, ahead=None):
        for lane in lane_starts:
            for n in range(modes):
                first = sub_buf[src, n, :, pl.ds(lane, LANES)] * rows_of(c_all[src], n, lane)
                if ahead is not None:
                    first = first * rows_of(ahead, n, lane)
                g_buf[n, :, pl.ds(lane, LANES)] = first

    def finish(src, begin, end, own):
        for lane in lane_starts:
            lam = [rows_of(lam_buf[src], n, lane) for n in range(modes)]

            def step(i, state, lam=lam, lane=lane):
                here = pl.ds(pl.multiple_of(i * 2 * SUB, 2 * SUB), 2 * SUB)
                gate = q_all[src, here, pl.ds(lane, LANES)].astype(F32)
                if own:
                    local = [y_buf[2 * i + o, :, pl.ds(lane, LANES)] for o in range(2)]
                else:
                    both = l_all[src, here, pl.ds(lane, LANES)].astype(F32)
                    local = [both[:SUB], both[SUB:]]
                pair = []
                for o in range(2):
                    pair.append(tree(list(state) + [local[o]]))
                    state = tuple(l * h for l, h in zip(lam, state))
                gathered[src, here, pl.ds(lane, LANES)] = (gate * jnp.concatenate(pair, axis=0)).astype(BF16)
                return state

            first = tuple(g_buf[n, :, pl.ds(lane, LANES)] for n in range(modes))
            last = lax.fori_loop(begin // 2, end // 2, step, first, unroll=2)
            for n in range(modes):
                g_buf[n, :, pl.ds(lane, LANES)] = last[n]

    def project(begin, end):
        projected = jnp.broadcast_to(bias_ref[...], ((end - begin) * SUB, channels))
        for yy in range(NY):
            projected = projected + jnp.dot(
                gathered[yy, rows(begin, end), :], w_buf[pl.ds(yy * channels, channels), :], preferred_element_type=F32
            )
        for i in range(end - begin):
            for lane in lane_starts:
                o_buf[lane // LANES, pl.ds(begin + i, SUB, stride=steps), :] = projected[
                    i * SUB : (i + 1) * SUB, lane : lane + LANES
                ]

    def late(first_late):
        for j in range(first_late, CHUNKS):
            finish(y, j * part, (j + 1) * part, True)
            for copy in late_hops(j):
                copy.start()

    start_carry(y, jnp.exp(-decay * jnp.where(lead, spans[1][1], spans[0][1]).astype(F32)))

    @pl.when(lead)
    def _():
        late(LEAD_EARLY)

    @pl.when(~lead)
    def _():
        late(LAG_EARLY)

    start_carry(y)
    finish(y, *spans[0], True)

    @pl.when(lead)
    def _():
        finish(y, *spans[1], True)

    for t in range(2):
        ring_finish(t, 0)

    @pl.when(lead)
    def _():
        for t in range(2):
            ring_finish(t, 1)

    for src in others:
        small_wait(1, c_all, src)
        start_carry(src)
        finish(src, *spans[0], False)

        @pl.when(lead)
        def _(src=src):
            finish(src, *spans[1], False)

    loads[6].wait()
    loads[7].wait()
    project(*spans[0])

    @pl.when(lead)
    def _():
        project(*spans[1])

    def project_late(first_late):
        for j in range(first_late, CHUNKS, 2):
            end = min(j + 2, CHUNKS)
            for i in range(j, end):
                for src in others:
                    piece = gathered.at[src, rows(i * part, (i + 1) * part)]
                    remote(piece, piece, late_send.at[0, i], late_recv.at[src, i], mate).wait_recv()
            project(j * part, end * part)

    @pl.when(lead)
    def _():
        project_late(LEAD_EARLY)

    @pl.when(~lead)
    def _():
        project_late(LAG_EARLY)

    for lane in lane_starts:
        out_ref[:, pl.ds(lane, LANES)] = o_buf[lane // LANES].astype(BF16)

    def sent(copies):
        for copy in copies:
            copy.wait_send()

    sent(small_hops(0, d_all, y) + small_hops(1, c_all, y))
    for t in range(2):
        sent(own_hops(t, 0) + forward_hops(t, 0))
    for j in range(LEAD_EARLY, CHUNKS):
        sent(late_hops(j))

    @pl.when(lead)
    def _():
        for t in range(2):
            sent(own_hops(t, 1) + forward_hops(t, 1))

    @pl.when(~lead)
    def _():
        for j in range(LAG_EARLY, LEAD_EARLY):
            sent(late_hops(j))

    for k in range(1, NZ):
        @pl.when(z + k < NZ)
        def _(k=k):
            state_copy(z, z + k).wait_send()

        @pl.when((z >= k) & needs_total)
        def _(k=k):
            state_copy(z, z - k).wait_send()
    for k in range(1, NX):
        @pl.when(x + k < NX)
        def _(k=k):
            for cc in range(NC):
                total_copy(x, x + k, cc).wait_send()


def layer(q_gate, k_gate, value, decay, residue, skip, out_weight, out_bias):
    tokens, channels = q_gate.shape
    modes = decay.shape[0]
    steps = tokens // SUB
    dma = pltpu.SemaphoreType.DMA
    regular = pltpu.SemaphoreType.REGULAR
    state = (modes, channels)
    by_lane = (channels // LANES, tokens, LANES)
    by_sublane = (modes, SUB, channels)
    any_spec = pl.BlockSpec(memory_space=pl.ANY)
    shapes = [
        (state, F32), (state, F32), ((1, channels), F32), ((1, channels), F32),
        ((tokens, channels), BF16), ((tokens, channels), BF16), ((tokens, channels), BF16),
        (out_weight.shape, BF16), (by_lane, F32), (by_lane, F32),
        ((steps, SUB, channels), F32), (by_sublane, F32),
        ((NY,) + state, F32), ((NY,) + by_sublane, F32), (by_sublane, F32),
        ((NY, tokens, channels), BF16), ((NY, tokens, channels), BF16),
        ((NY,) + state, F32), ((NY,) + state, F32),
        ((NY, tokens, channels), BF16),
        ((NZ,) + state, F32), ((NC, NX) + state, F32),
        (state, F32), (state, F32), (state, F32), (state, F32),
        (by_lane, F32),
    ]
    return pl.pallas_call(
        kernel,
        out_shape=pltpu.VMEM((tokens, channels), BF16),
        in_specs=[any_spec] * 8,
        out_specs=pl.BlockSpec(memory_space=pltpu.VMEM),
        scratch_shapes=[pltpu.VMEM(*shape) for shape in shapes]
        + [
            dma((8,)), regular, regular((NY,)), regular((NZ,)), regular((NX, NC)), dma((NZ,)), dma((NZ,)), dma((NX, NC)), dma((NC, NX)),
            dma((2,)), dma((2,)), dma((NY - 1, CHUNKS)), dma((NY, CHUNKS)),
            dma((2, NY - 1)), dma((2, NY)), dma((2, 2, 6)), dma((2, 2, NY, 2)),
        ],
        compiler_params=pltpu.CompilerParams(
            collective_id=0, has_side_effects=True, vmem_limit_bytes=62 * 2**20
        ),
        name="layer",
    )(q_gate, k_gate, value, decay, residue, skip.reshape(1, -1), out_weight, out_bias.reshape(1, -1))


def solution(mesh):
    return jax.shard_map(
        layer,
        mesh=mesh,
        in_specs=(
            P("seq", "chan"),
            P("seq", "chan"),
            P("seq", "chan"),
            P(None, "chan"),
            P(None, "chan"),
            P("chan"),
            P(None, "chan"),
            P("chan"),
        ),
        out_specs=P("seq", "chan"),
        check_vma=False,
    )
```
